32 devices in a mesh: dp: 4 (over z), ctx: 2 (over x), tensor: 4 (over y, core).
Axes of the slice: x: 2, y: 2, z: 4, core: 2. Of those that a mesh axis runs over, the one named last changes fastest.
Arguments:
- inputs: bfloat16 [4, 1024, 768], P('dp', 'ctx'), may hold values from -6 to 6
- gain_attention: float32 [768], replicated, may hold values from 0.5 to 1.5
- w_query: bfloat16 [768, 768], P(('dp', 'ctx'), 'tensor'), may hold values from -0.21875 to 0.21875
- w_key: bfloat16 [768, 768], P(('dp', 'ctx'), 'tensor'), may hold values from -0.21875 to 0.21875
- w_value: bfloat16 [768, 768], P(('dp', 'ctx'), 'tensor'), may hold values from -0.21875 to 0.21875
- w_output: bfloat16 [768, 768], P(('dp', 'ctx'), 'tensor'), may hold values from -1.5 to 1.5
- bias_table: float32 [32, 12], P(None, 'tensor'), may hold values from -4 to 4
- bucket_start: int32 [32], replicated, may hold values from 0 to 1023, as said below
- gain_experts: float32 [768], replicated, may hold values from 0.5 to 1.5
- w_router: bfloat16 [768, 8], replicated, may hold values from -0.15625 to 0.15625
- w_up: bfloat16 [8, 768, 3072], P(('dp', 'ctx'), None, 'tensor'), may hold values from -0.21875 to 0.21875
- w_down: bfloat16 [8, 3072, 768], P(('dp', 'ctx'), 'tensor'), may hold values from -0.15625 to 0.15625
- expert_ids: int32 [4, 1024, 2], P('dp', 'ctx'), may hold values from 0 to 7, as said below
- slot_index: int32 [4, 1024, 2], P('dp', 'ctx'), may hold values from -1 to 159, as said below
- cotangent: bfloat16 [4, 1024, 768], P('dp', 'ctx'), may hold values from -6 to 6
Outputs:
- layer_out: bfloat16 [4, 1024, 768], P('dp', 'ctx')
- grad_inputs: float32 [4, 1024, 768], P('dp', 'ctx')
- grad_gain_attention: float32 [768], replicated
- grad_w_query: float32 [768, 768], P(None, 'tensor')
- grad_w_key: float32 [768, 768], P(None, 'tensor')
- grad_w_value: float32 [768, 768], P(None, 'tensor')
- grad_w_output: float32 [768, 768], P(None, 'tensor')
- grad_bias_table: float32 [32, 12], P(None, 'tensor')
- grad_gain_experts: float32 [768], replicated
- grad_router: float32 [768, 8], replicated
- grad_w_up: float32 [8, 768, 3072], P(('dp', 'ctx'), None, 'tensor')
- grad_w_down: float32 [8, 3072, 768], P(('dp', 'ctx'), 'tensor')
The draws below stay inside these ranges and needn't reach their ends.
Inputs may be any that keep to these rules, and one draw needn't show every extreme that they name: `expert_ids`: each token names 2 different experts. `slot_index`: take the 512 tokens of one index of dp and ctx by sequence, then position, then choice. The choices of these tokens that name one expert get slots 0, 1, 2 and so on in that order; those past 160 get -1. In every draw some expert gets all 160 slots from every index of dp and ctx. bucket_start[b] = b for b <= 16, strictly increasing after that, and bucket_start[31] = 1023.
All inputs are finite; a program needn't handle non-finite values.
Results may differ from the reference program's by a relative error of at most 0.017.
Values may be sent and summed in bfloat16 or wider, within the bound.
A program may use at most 128 MiB of HBM per device.

```python
from functools import partial
import jax
import jax.numpy as jnp
from jax import lax

D = 768
HEADS = 12
HEAD_DIM = 64
FF = 3072
BUCKETS = 32
TOP = 2
SEQ_DEV = 512
SEQS = 1
HH = 768
LEN = 1024
BATCH = 4
EXPERTS = 8
C_SEND = 160


def shared_routes(key):
    key_weight, key_hot, key_first, key_second, key_other = jax.random.split(key, 5)
    weights = jax.random.randint(key_weight, (EXPERTS,), 2, 7)
    hottest = jax.random.randint(key_hot, (), 0, EXPERTS)
    weights = jnp.where(jnp.arange(EXPERTS) == hottest, 16, weights)
    bounds = jnp.cumsum(weights)
    total = bounds[EXPERTS - 1]
    first_draw = jax.random.randint(key_first, (BATCH, LEN), 0, total)
    second_draw = jax.random.randint(key_second, (BATCH, LEN), 0, total)
    first = jnp.sum((first_draw[..., None] >= bounds[None, None, :]).astype(jnp.int32), axis=-1)
    second = jnp.sum((second_draw[..., None] >= bounds[None, None, :]).astype(jnp.int32), axis=-1)
    other = (first + jax.random.randint(key_other, (BATCH, LEN), 1, EXPERTS)) % EXPERTS
    second = jnp.where(second == first, other, second)
    return jnp.stack([first, second], axis=-1).astype(jnp.int32)


def draw_expert_ids(key, part):
    return shared_routes(key)


def draw_slot_index(key, part):
    routes = shared_routes(key)
    groups = LEN // SEQ_DEV
    owners = BATCH // SEQS
    grouped = routes.reshape(owners, SEQS, groups, SEQ_DEV, TOP).transpose(0, 2, 1, 3, 4).reshape(owners * groups, SEQS * SEQ_DEV * TOP)
    hits = (grouped[:, :, None] == jnp.arange(EXPERTS, dtype=jnp.int32)[None, None, :]).astype(jnp.int32)
    earlier = jnp.cumsum(hits, axis=1) - hits
    order = jnp.sum(earlier * hits, axis=-1)
    order = jnp.where(order < C_SEND, order, -1)
    return order.reshape(owners, groups, SEQS, SEQ_DEV, TOP).transpose(0, 2, 1, 3, 4).reshape(BATCH, LEN, TOP).astype(jnp.int32)


def draw_bucket_start(key, part):
    key = jax.random.fold_in(key, 5)
    half = BUCKETS // 2
    picked = jax.random.permutation(key, LEN - half - 2)[:BUCKETS - half - 2] + half + 1
    last = jnp.full((1,), LEN - 1, dtype=jnp.int32)
    return jnp.concatenate([jnp.arange(half + 1, dtype=jnp.int32), jnp.sort(picked).astype(jnp.int32), last]).astype(jnp.int32)


def block_levels(key, extent, shards, low, high):
    loudness = 1.0
    for axis_at, shards_of in shards:
        heights = jax.random.uniform(jax.random.fold_in(jax.random.fold_in(key, 6), axis_at), (shards_of,), jnp.float32, low / len(shards), high / len(shards))
        loudness = loudness * jnp.repeat(jnp.exp(heights), extent[axis_at] // shards_of).reshape((-1,) + (1,) * (len(extent) - 1 - axis_at))
    return loudness


def noise(stream_key, extent, deviation, most, cuts=(), kind=jnp.bfloat16):
    array = deviation * jax.random.normal(stream_key, extent, jnp.float32)
    if cuts:
        array = array * block_levels(stream_key, extent, cuts, -0.22, 0.18)
    return jnp.clip(array, -most, most).astype(kind)


def setup_inputs(seed: int = 0) -> dict:
    splits = jax.random.split(jax.random.key(seed), 16)
    return {
        "inputs": noise(splits[0], (BATCH, LEN, D), 1.0, 6.0, ((0, 4), (1, 2))),
        "gain_attention": jnp.clip(1.0 + 0.1 * jax.random.normal(splits[1], (D,), jnp.float32), 0.5, 1.5),
        "w_query": noise(splits[2], (D, HH), D ** -0.5, 0.21875, ((0, 8), (1, 4))),
        "w_key": noise(splits[3], (D, HH), D ** -0.5, 0.21875, ((0, 8), (1, 4))),
        "w_value": noise(splits[4], (D, HH), D ** -0.5, 0.21875, ((0, 8), (1, 4))),
        "w_output": noise(splits[5], (D, HH), (max(HH // 48, 2)) ** -0.5, 1.5, ((0, 8), (1, 4))),
        "bias_table": noise(splits[6], (BUCKETS, HEADS), 1.0, 4.0, ((1, 4),), jnp.float32),
        "bucket_start": draw_bucket_start(jax.random.fold_in(splits[15], 71), 0),
        "gain_experts": jnp.clip(1.0 + 0.1 * jax.random.normal(splits[8], (D,), jnp.float32), 0.5, 1.5),
        "w_router": noise(splits[9], (D, EXPERTS), (2 * D) ** -0.5, 0.15625),
        "w_up": noise(splits[10], (EXPERTS, D, FF), D ** -0.5, 0.21875, ((0, 8), (2, 4))),
        "w_down": noise(splits[11], (EXPERTS, FF, D), (FF // 2) ** -0.5, 0.15625, ((0, 8), (1, 4))),
        "expert_ids": draw_expert_ids(jax.random.fold_in(splits[15], 71), 0),
        "slot_index": draw_slot_index(jax.random.fold_in(splits[15], 71), 0),
        "cotangent": noise(splits[14], (BATCH, LEN, D), 1.0, 6.0, ((0, 4), (1, 2))),
    }


EPS = 1e-06
HIGHEST = lax.Precision.HIGHEST
MASKED = -1e+30

@jax.custom_vjp
def low(v):
    return lax.optimization_barrier(v.astype(jnp.bfloat16)).astype(jnp.float32)

@jax.custom_vjp
def low_back(v):
    return v

def low_keep(v):
    return (low(v), None)

def low_pass(kept, grad):
    return (grad,)

def back_keep(v):
    return (v, None)

def back_low(kept, grad):
    return (low(grad),)
low.defvjp(low_keep, low_pass)
low_back.defvjp(back_keep, back_low)

def rms_norm(value, gain):
    scale = lax.rsqrt(lax.optimization_barrier(jnp.mean(value * value, axis=-1, keepdims=True)) + EPS)
    return value * scale * gain

def forward(expert_ids, slot_index, bucket_start, source, gain_one, query_w, key_w, value_w, output_w, table, gain_two, router_w, up_w, down_w):
    normed_one = low(rms_norm(source, gain_one))

    def project(weight):
        made = jnp.einsum('bld,dh->blh', normed_one, weight, precision=HIGHEST)
        return low_back(low(made)).reshape(BATCH, LEN, HEADS, HEAD_DIM)
    query = project(query_w)
    keys = project(key_w)
    values = project(value_w)
    position = jnp.arange(LEN, dtype=jnp.int32)
    distance = position[:, None] - position[None, :]
    bucket = jnp.searchsorted(bucket_start, distance, side='right').astype(jnp.int32) - 1
    bucket = jnp.maximum(bucket, 0)
    bias = jnp.transpose(jnp.take(table, bucket, axis=0), (2, 0, 1))
    causal = distance >= 0

    def attend(pieces):
        one_query, one_keys, one_values = pieces
        logits = jnp.einsum('qhd,khd->hqk', one_query, one_keys, precision=HIGHEST) * HEAD_DIM ** (-0.5)
        logits = low_back(logits + bias)
        shares = jax.nn.softmax(jnp.where(causal[None], logits, MASKED), axis=-1)
        mixed = jnp.einsum('hqk,khd->qhd', low(shares), one_values, precision=HIGHEST)
        return low_back(low(mixed))
    mixed = lax.map(jax.checkpoint(attend), (query, keys, values)).reshape(BATCH, LEN, HEADS * HEAD_DIM)
    branch = low_back(jnp.einsum('blh,dh->bld', mixed, output_w, precision=HIGHEST))
    hidden_one = source + branch
    normed_two = low(rms_norm(hidden_one, gain_two))
    router_logits = low_back(jnp.einsum('bld,de->ble', normed_two, router_w, precision=HIGHEST))
    chosen = jnp.take_along_axis(router_logits, expert_ids, axis=-1)
    gates = jax.nn.softmax(chosen, axis=-1)
    batch_pos = jnp.arange(BATCH, dtype=jnp.int32)[:, None, None]
    seq_pos = jnp.arange(LEN, dtype=jnp.int32)[None, :, None]
    anchor = batch_pos // SEQS * (LEN // SEQ_DEV) + seq_pos // SEQ_DEV
    rows_all = EXPERTS * EXPERTS * C_SEND
    kept = slot_index >= 0
    target = jnp.where(kept, expert_ids * (EXPERTS * C_SEND) + anchor * C_SEND + slot_index, rows_all).astype(jnp.int32)
    spread = jnp.broadcast_to(normed_two[:, :, None, :], (BATCH, LEN, TOP, D)).reshape(BATCH * LEN * TOP, D)
    buffer = jnp.zeros((rows_all, D), spread.dtype).at[target.reshape(-1)].set(spread, mode='drop')
    buffer = buffer.reshape(EXPERTS, EXPERTS * C_SEND, D)

    def expert(pieces):
        rows, up_one, down_one = pieces
        before = low_back(jnp.einsum('rd,df->rf', rows, up_one, precision=HIGHEST))
        activated = low(jax.nn.gelu(before))
        return low_back(low(jnp.einsum('rf,fd->rd', activated, down_one, precision=HIGHEST)))
    produced = lax.map(jax.checkpoint(expert), (buffer, up_w, down_w)).reshape(rows_all, D)
    safe = jnp.minimum(target, rows_all - 1).astype(jnp.int32)
    picked = jnp.where(kept[..., None], jnp.take(produced, safe, axis=0), 0.0)
    mixture = lax.optimization_barrier(jnp.sum(gates[..., None] * picked, axis=2))
    return hidden_one + mixture

def reference(inputs, gain_attention, w_query, w_key, w_value, w_output, bias_table, bucket_start, gain_experts, w_router, w_up, w_down, expert_ids, slot_index, cotangent):
    floats = (inputs.astype(jnp.float32), gain_attention.astype(jnp.float32), w_query.astype(jnp.float32), w_key.astype(jnp.float32), w_value.astype(jnp.float32), w_output.astype(jnp.float32), bias_table.astype(jnp.float32), gain_experts.astype(jnp.float32), w_router.astype(jnp.float32), w_up.astype(jnp.float32), w_down.astype(jnp.float32))
    result, pullback = jax.vjp(partial(forward, expert_ids, slot_index, bucket_start), *floats)
    grads = pullback(cotangent.astype(jnp.float32))
    return (result.astype(jnp.bfloat16), grads[0], grads[1], grads[2], grads[3], grads[4], grads[5], grads[6], grads[7], grads[8], grads[9], grads[10])
```

```python
import functools

import jax
import jax.numpy as jnp
from jax import lax
from jax.experimental import pallas as pl
from jax.experimental.pallas import tpu as pltpu
from jax.sharding import PartitionSpec as P

EPS = 1e-06
MASKED = -1e30
SUB = 128
F32 = jnp.float32
BF16 = jnp.bfloat16


def dot(a, b, ca=1, cb=0):
    return lax.dot_general(a, b, (((ca,), (cb,)), ((), ())), preferred_element_type=F32)


def lane_distance(delta, rows, v):
    span = 2 * rows
    v = jnp.where(v > span - SUB, v - span, v)
    return delta * rows + rows - SUB - v


def bias_band(delta, rows, heads, starts_ref, table_ref, band_ref):
    span = 2 * rows
    far = lane_distance(delta, rows, lax.broadcasted_iota(jnp.int32, (8, span), 1))
    lines = [jnp.full((8, span), MASKED, F32) for _ in range(heads)]
    for b in range(table_ref.shape[0]):
        reached = far >= starts_ref[b]
        for h in range(heads):
            lines[h] = jnp.where(reached, table_ref[b, h], lines[h])
    for h in range(heads):
        wide = jnp.broadcast_to(lines[h][0:1], (SUB, span))
        band_ref[h] = pltpu.roll(wide, 0, 1, stride=1, stride_axis=0)


def forward_kernel(
    heads, ctx_ref, starts_ref, table_ref, q_ref, k_ref, v_ref,
    mixed_ref, wide_ref, log_ref, band_ref, peak_ref, total_ref,
):
    rows = q_ref.shape[0]
    dim = q_ref.shape[1] // heads
    me = ctx_ref[0]
    peak_ref[...] = jnp.full_like(peak_ref, MASKED)
    total_ref[...] = jnp.zeros_like(total_ref)
    wide_ref[...] = jnp.zeros_like(wide_ref)

    def step_fn(step, carry):
        bias_band(me - step, rows, heads, starts_ref, table_ref, band_ref)
        at = pl.multiple_of(step * rows, rows)
        for h in range(heads):
            cols = slice(h * dim, (h + 1) * dim)
            keys = k_ref[pl.ds(at, rows), cols]
            values = v_ref[pl.ds(at, rows), cols]
            for a in range(rows // SUB):
                mine = slice(a * SUB, (a + 1) * SUB)
                off = rows - SUB - SUB * a
                query = q_ref[mine, cols] * BF16(dim ** -0.5)
                logits = dot(query, keys, 1, 1) + band_ref[h, :, off : off + rows]
                old = peak_ref[h, mine, :]
                new = jnp.maximum(old, jnp.max(logits, axis=1, keepdims=True))
                shares = jnp.exp(logits - new)
                shrink = jnp.exp(old - new)
                peak_ref[h, mine, :] = new
                total_ref[h, mine, :] = total_ref[h, mine, :] * shrink + jnp.sum(
                    shares, axis=1, keepdims=True
                )
                wide_ref[mine, cols] = wide_ref[mine, cols] * shrink + dot(
                    shares.astype(BF16), values
                )
        return carry

    lax.fori_loop(0, me + 1, step_fn, 0)
    for h in range(heads):
        cols = slice(h * dim, (h + 1) * dim)
        total = total_ref[h]
        mixed = wide_ref[:, cols] / total
        wide_ref[:, cols] = mixed
        mixed_ref[:, cols] = mixed.astype(BF16)
        log_ref[:, h : h + 1] = peak_ref[h] + jnp.log(total)


def backward_kernel(
    heads, ctx_ref, starts_ref, table_ref, q_ref, k_ref, v_ref, g_ref, wide_ref, log_ref,
    dq_ref, dk_ref, dv_ref, diag_ref, band_ref, sums_ref, dlogit_ref, share_ref, acc_ref,
):
    rows = q_ref.shape[0]
    span = 2 * rows
    dim = q_ref.shape[1] // heads
    me = ctx_ref[0]
    dk_ref[...] = jnp.zeros_like(dk_ref)
    dv_ref[...] = jnp.zeros_like(dv_ref)
    diag_ref[...] = jnp.zeros_like(diag_ref)
    acc_ref[...] = jnp.zeros_like(acc_ref)

    def step_fn(step, carry):
        delta = me - step
        bias_band(delta, rows, heads, starts_ref, table_ref, band_ref)
        at = pl.multiple_of(step * rows, rows)
        for h in range(heads):
            cols = slice(h * dim, (h + 1) * dim)
            keys = k_ref[pl.ds(at, rows), cols]
            values = v_ref[pl.ds(at, rows), cols]
            sums_ref[...] = jnp.zeros_like(sums_ref)
            for a in range(rows // SUB):
                mine = slice(a * SUB, (a + 1) * SUB)
                off = rows - SUB - SUB * a
                query = q_ref[mine, cols] * BF16(dim ** -0.5)
                grad = g_ref[mine, cols]
                inner = jnp.sum(grad.astype(F32) * wide_ref[mine, cols], axis=1, keepdims=True)
                logits = dot(query, keys, 1, 1) + band_ref[h, :, off : off + rows]
                shares = jnp.exp(logits - log_ref[mine, h : h + 1])
                dlogits = shares * (dot(grad, values, 1, 1) - inner)
                sums_ref[:, off : off + rows] += dlogits
                low = dlogits.astype(BF16)
                share_ref[mine, :] = shares.astype(BF16)
                dlogit_ref[mine, :] = low
                acc_ref[mine, cols] += dot(low, keys)
            dk_ref[pl.ds(at, rows), cols] = (
                dot(dlogit_ref[...], q_ref[:, cols], 0, 0) * dim ** -0.5
            ).astype(BF16)
            dv_ref[pl.ds(at, rows), cols] = dot(share_ref[...], g_ref[:, cols], 0, 0).astype(BF16)
            folded = sums_ref[...]
            width = SUB // 2
            while width >= 8:
                folded = folded[:width] + pltpu.roll(folded[width:], span - width, 1)
                width //= 2
            diag_ref[h, delta] = folded
        return carry

    lax.fori_loop(0, me + 1, step_fn, 0)
    dq_ref[...] = (acc_ref[...] * dim ** -0.5).astype(BF16)


def specs(*kinds):
    return [pl.BlockSpec(memory_space=pltpu.SMEM if k == "s" else pltpu.VMEM) for k in kinds]


def attend_forward(me, starts, table, query, keys, values):
    rows, width = query.shape
    heads = table.shape[1]
    return pl.pallas_call(
        functools.partial(forward_kernel, heads),
        out_shape=(
            jax.ShapeDtypeStruct((rows, width), BF16),
            jax.ShapeDtypeStruct((rows, width), F32),
            jax.ShapeDtypeStruct((rows, heads), F32),
        ),
        in_specs=specs(*"sssvvv"),
        out_specs=tuple(specs(*"vvv")),
        scratch_shapes=[
            pltpu.VMEM((heads, SUB, 2 * rows), F32),
            pltpu.VMEM((heads, rows, 1), F32),
            pltpu.VMEM((heads, rows, 1), F32),
        ],
        compiler_params=pltpu.CompilerParams(vmem_limit_bytes=40 * 2**20),
        name="attend_forward",
    )(me, starts, table, query, keys, values)


def attend_backward(me, starts, table, query, keys, values, grad, wide, logs):
    rows, width = query.shape
    length = keys.shape[0]
    heads = table.shape[1]
    return pl.pallas_call(
        functools.partial(backward_kernel, heads),
        out_shape=(
            jax.ShapeDtypeStruct((rows, width), BF16),
            jax.ShapeDtypeStruct((length, width), BF16),
            jax.ShapeDtypeStruct((length, width), BF16),
            jax.ShapeDtypeStruct((heads, length // rows, 8, 2 * rows), F32),
        ),
        in_specs=specs(*"sssvvvvvv"),
        out_specs=tuple(specs(*"vvvv")),
        scratch_shapes=[
            pltpu.VMEM((heads, SUB, 2 * rows), F32),
            pltpu.VMEM((SUB, 2 * rows), F32),
            pltpu.VMEM((rows, rows), BF16),
            pltpu.VMEM((rows, rows), BF16),
            pltpu.VMEM((rows, width), F32),
        ],
        compiler_params=pltpu.CompilerParams(vmem_limit_bytes=40 * 2**20),
        name="attend_backward",
    )(me, starts, table, query, keys, values, grad, wide, logs)


def table_grad(diag, starts):
    heads, blocks, sub, span = diag.shape
    delta = lax.broadcasted_iota(jnp.int32, (blocks, sub, span), 0)
    row = lax.broadcasted_iota(jnp.int32, (blocks, sub, span), 1)
    lane = lax.broadcasted_iota(jnp.int32, (blocks, sub, span), 2)
    far = lane_distance(delta, span // 2, lane) + row
    later = jnp.concatenate([starts[1:], jnp.full((1,), 2**30, jnp.int32)])
    inside = (far[None] >= starts[:, None, None, None]) & (far[None] < later[:, None, None, None])
    return jnp.sum(
        jnp.where(inside[:, None], diag[None], 0.0), axis=(2, 3, 4)
    )


def hi_lo(x):
    hi = x.astype(BF16)
    return hi, (x - hi.astype(F32)).astype(BF16)


def norm_scale(value):
    return lax.rsqrt(jnp.mean(value * value, axis=-1, keepdims=True) + EPS)


def norm_backward(value, scale, gain, grad_normed):
    scaled = grad_normed * gain
    grad_value = scale * scaled - value * scale**3 * jnp.mean(
        value * scaled, axis=-1, keepdims=True
    )
    return grad_value, jnp.sum(grad_normed * value * scale, axis=0)


def sum_groups(grad):
    part = lax.psum_scatter(grad.astype(BF16), ("dp", "ctx"), scatter_dimension=0, tiled=True)
    return lax.all_gather(part, ("dp", "ctx"), axis=0, tiled=True).astype(F32)


def on_device(
    inputs, gain_attention, w_query, w_key, w_value, w_output, bias_table, bucket_start,
    gain_experts, w_router, w_up, w_down, expert_ids, slot_index, cotangent,
):
    sequences, rows, width = inputs.shape
    tokens = sequences * rows
    experts = w_router.shape[1]
    top = expert_ids.shape[2]
    capacity = 5 * tokens * top // (4 * experts)
    heads = bias_table.shape[1]
    split = lax.axis_size("tensor")
    ctxs = lax.axis_size("ctx")
    at_tensor = lax.axis_index("tensor")
    at_ctx = lax.axis_index("ctx")
    me = at_ctx.astype(jnp.int32).reshape(1)
    part = tokens // split
    slots = capacity // split
    shard_rows = experts * slots
    groups = ("dp", "ctx")

    def my_tokens(x):
        return lax.dynamic_slice_in_dim(x, at_tensor * part, part, 0)

    def gather_tensor(x):
        return lax.all_gather(x, "tensor", axis=0, tiled=True)

    def scatter_tensor(x):
        return lax.psum_scatter(x.astype(BF16), "tensor", scatter_dimension=0, tiled=True)

    def exchange(x):
        return lax.all_to_all(x, groups, split_axis=0, concat_axis=0, tiled=True)

    route = expert_ids.reshape(tokens, top)
    place = slot_index.reshape(tokens, top)
    local = place - at_tensor * slots
    inside = (place >= 0) & (local >= 0) & (local < slots)
    row_of = jnp.where(inside, route * slots + local, -1)
    spots = jnp.arange(shard_rows, dtype=jnp.int32)
    hits = [row_of[:, k : k + 1] == spots[None, :] for k in range(top)]
    ones = [h.astype(BF16) for h in hits]
    any_hit = sum(ones[1:], ones[0])
    cot = cotangent.reshape(tokens, width)

    qkv_w = lax.all_gather(
        jnp.concatenate([w_query, w_key, w_value], axis=1), groups, axis=0, tiled=True
    )
    output_w = lax.all_gather(w_output, groups, axis=0, tiled=True)
    cot_rows = gather_tensor(exchange(dot(any_hit, cot, 0, 0).astype(BF16)))
    source = inputs.astype(F32).reshape(tokens, width)
    scale_one = norm_scale(source)
    normed_one = (source * scale_one * gain_attention).astype(BF16)
    hh = w_query.shape[1]
    qkv = dot(normed_one, qkv_w).astype(BF16).reshape(sequences, rows, 3 * hh)
    kv_all = lax.all_gather(qkv[:, :, hh:], "ctx", axis=1, tiled=True)
    seen = [
        attend_forward(
            me, bucket_start, bias_table,
            qkv[b, :, :hh], kv_all[b, :, :hh], kv_all[b, :, hh:],
        )
        for b in range(sequences)
    ]
    mixed = jnp.concatenate([s[0] for s in seen], axis=0)
    source_mine = my_tokens(source)
    hidden = source_mine + scatter_tensor(dot(mixed, output_w, 1, 1)).astype(F32)
    scale_two = norm_scale(hidden)
    normed_mine = (hidden * scale_two * gain_experts).astype(BF16)
    normed_two = gather_tensor(normed_mine)

    router_logits = dot(normed_two, w_router)
    picks = route[:, :, None] == jnp.arange(experts, dtype=jnp.int32)[None, None, :]
    chosen = jnp.sum(jnp.where(picks, router_logits[:, None, :], 0.0), axis=-1)
    gates = jax.nn.softmax(chosen, axis=-1)
    row_gate = sum(
        jnp.sum(jnp.where(hits[k], gates[:, k : k + 1], 0.0), axis=0) for k in range(top)
    )

    gate_hi, gate_lo = hi_lo(row_gate[:, None])
    sent = jnp.concatenate(
        [
            dot(any_hit, normed_two, 0, 0).astype(BF16),
            jnp.broadcast_to(gate_hi, (shard_rows, 64)),
            jnp.broadcast_to(gate_lo, (shard_rows, 64)),
        ],
        axis=1,
    )
    arrived = gather_tensor(exchange(sent))
    buffer = arrived[:, :width]
    gate_rows = arrived[:, width : width + 1].astype(F32) + arrived[
        :, width + 64 : width + 65
    ].astype(F32)
    grad_produced = (gate_rows * cot_rows.astype(F32)).astype(BF16)
    up, down = w_up[0], w_down[0]
    before = dot(buffer, up)
    activated, gelu_pullback = jax.vjp(jax.nn.gelu, before)
    activated = activated.astype(BF16)
    returned = exchange(scatter_tensor(dot(activated, down)))
    grad_before = gelu_pullback(dot(grad_produced, down, 1, 1))[0].astype(BF16)
    grad_returned = exchange(scatter_tensor(dot(grad_before, up, 1, 1)))
    grad_down = dot(activated, grad_produced, 0, 0)
    grad_up = dot(buffer, grad_before, 0, 0)

    cot32 = cot.astype(F32)
    picked = [dot(one, returned) for one in ones]
    mixture = sum(gates[:, k : k + 1] * picked[k] for k in range(top))
    gate_part = jnp.stack([jnp.sum(cot32 * picked[k], axis=-1) for k in range(top)], axis=1)
    part_hi, part_lo = hi_lo(gate_part)
    summed = scatter_tensor(
        jnp.concatenate(
            [
                mixture.astype(BF16),
                dot(any_hit, grad_returned).astype(BF16),
                jnp.pad(jnp.concatenate([part_hi, part_lo], axis=1), ((0, 0), (0, 128 - 2 * top))),
            ],
            axis=1,
        )
    ).astype(F32)
    result = hidden + summed[:, :width]
    layer_out = gather_tensor(result.astype(BF16))
    grad_gates = (
        summed[:, 2 * width : 2 * width + top] + summed[:, 2 * width + top : 2 * width + 2 * top]
    )
    gates_mine = my_tokens(gates)
    grad_chosen = gates_mine * (
        grad_gates - jnp.sum(gates_mine * grad_gates, axis=-1, keepdims=True)
    )
    grad_logits = jnp.sum(
        jnp.where(my_tokens(picks), grad_chosen[:, :, None], 0.0), axis=1
    ).astype(BF16)
    grad_router = dot(normed_mine, grad_logits, 0, 0)
    grad_normed_two = summed[:, width : 2 * width] + dot(grad_logits, w_router, 1, 1)
    grad_back, grad_gain_two = norm_backward(hidden, scale_two, gain_experts, grad_normed_two)
    grad_hidden = my_tokens(cot).astype(F32) + grad_back
    grad_branch = gather_tensor(grad_hidden.astype(BF16))

    grad_mixed = dot(grad_branch, output_w).astype(BF16).reshape(sequences, rows, hh)
    grad_output = sum_groups(dot(grad_branch, mixed, 0, 0))
    back = [
        attend_backward(
            me, bucket_start, bias_table,
            qkv[b, :, :hh], kv_all[b, :, :hh], kv_all[b, :, hh:],
            grad_mixed[b], seen[b][1], seen[b][2],
        )
        for b in range(sequences)
    ]
    kv_part = jnp.stack([jnp.concatenate([b[1], b[2]], axis=1) for b in back])
    kv_grad = lax.psum_scatter(kv_part, "ctx", scatter_dimension=1, tiled=True)
    qkv_grad = jnp.concatenate([jnp.stack([b[0] for b in back]), kv_grad], axis=2).reshape(
        tokens, 3 * hh
    )
    grad_table = sum(table_grad(b[3], bucket_start) for b in back)
    grad_normed_one = scatter_tensor(dot(qkv_grad, qkv_w, 1, 1)).astype(F32)
    grad_qkv_w = sum_groups(dot(normed_one, qkv_grad, 0, 0))
    grad_back_one, grad_gain_one = norm_backward(
        source_mine, my_tokens(scale_one), gain_attention, grad_normed_one
    )
    grad_inputs = gather_tensor((grad_hidden + grad_back_one).astype(BF16)).astype(F32)

    small = lax.psum(
        jnp.concatenate([grad_gain_one[:, None], grad_gain_two[:, None], grad_router], axis=1).T,
        ("dp", "ctx", "tensor"),
    )
    grad_table = lax.psum(grad_table, groups)
    return (
        layer_out.reshape(sequences, rows, width),
        grad_inputs.reshape(sequences, rows, width),
        small[0],
        grad_qkv_w[:, :hh],
        grad_qkv_w[:, hh : 2 * hh],
        grad_qkv_w[:, 2 * hh :],
        grad_output,
        grad_table,
        small[1],
        small[2:].T,
        grad_up[None],
        grad_down[None],
    )


def solution(mesh):
    in_specs = (
        P("dp", "ctx", None),
        P(),
        P(("dp", "ctx"), "tensor"),
        P(("dp", "ctx"), "tensor"),
        P(("dp", "ctx"), "tensor"),
        P(("dp", "ctx"), "tensor"),
        P(None, "tensor"),
        P(),
        P(),
        P(),
        P(("dp", "ctx"), None, "tensor"),
        P(("dp", "ctx"), "tensor", None),
        P("dp", "ctx", None),
        P("dp", "ctx", None),
        P("dp", "ctx", None),
    )
    out_specs = (
        P("dp", "ctx", None),
        P("dp", "ctx", None),
        P(),
        P(None, "tensor"),
        P(None, "tensor"),
        P(None, "tensor"),
        P(None, "tensor"),
        P(None, "tensor"),
        P(),
        P(),
        P(("dp", "ctx"), None, "tensor"),
        P(("dp", "ctx"), "tensor", None),
    )
    return jax.shard_map(
        on_device, mesh=mesh, in_specs=in_specs, out_specs=out_specs, check_vma=False
    )
```

```python
import functools

import jax
import jax.numpy as jnp
from jax import lax
from jax.experimental import pallas as pl
from jax.experimental.pallas import tpu as pltpu
from jax.sharding import PartitionSpec as P

EPS = 1e-06
MASKED = -1e30
SUB = 128
F32 = jnp.float32
BF16 = jnp.bfloat16


def dot(a, b, ca=1, cb=0):
    return lax.dot_general(a, b, (((ca,), (cb,)), ((), ())), preferred_element_type=F32)


def lane_distance(delta, rows, v):
    span = 2 * rows
    v = jnp.where(v > span - SUB, v - span, v)
    return delta * rows + rows - SUB - v


def bias_band(delta, rows, heads, starts_ref, table_ref, band_ref):
    span = 2 * rows
    far = lane_distance(delta, rows, lax.broadcasted_iota(jnp.int32, (8, span), 1))
    lines = [jnp.full((8, span), MASKED, F32) for _ in range(heads)]
    for b in range(table_ref.shape[0]):
        reached = far >= starts_ref[b]
        for h in range(heads):
            lines[h] = jnp.where(reached, table_ref[b, h], lines[h])
    for h in range(heads):
        wide = jnp.broadcast_to(lines[h][0:1], (SUB, span))
        band_ref[h] = pltpu.roll(wide, 0, 1, stride=1, stride_axis=0)


def forward_kernel(
    heads, ctx_ref, starts_ref, table_ref, q_ref, k_ref, v_ref,
    mixed_ref, wide_ref, log_ref, band_ref, peak_ref, total_ref,
):
    rows = q_ref.shape[0]
    dim = q_ref.shape[1] // heads
    me = ctx_ref[0]
    peak_ref[...] = jnp.full_like(peak_ref, MASKED)
    total_ref[...] = jnp.zeros_like(total_ref)
    wide_ref[...] = jnp.zeros_like(wide_ref)

    def step_fn(step, carry):
        bias_band(me - step, rows, heads, starts_ref, table_ref, band_ref)
        at = pl.multiple_of(step * rows, rows)
        for h in range(heads):
            cols = slice(h * dim, (h + 1) * dim)
            keys = k_ref[pl.ds(at, rows), cols]
            values = v_ref[pl.ds(at, rows), cols]
            for a in range(rows // SUB):
                mine = slice(a * SUB, (a + 1) * SUB)
                off = rows - SUB - SUB * a
                query = q_ref[mine, cols] * BF16(dim ** -0.5)
                logits = dot(query, keys, 1, 1) + band_ref[h, :, off : off + rows]
                old = peak_ref[h, mine, :]
                new = jnp.maximum(old, jnp.max(logits, axis=1, keepdims=True))
                shares = jnp.exp(logits - new)
                shrink = jnp.exp(old - new)
                peak_ref[h, mine, :] = new
                total_ref[h, mine, :] = total_ref[h, mine, :] * shrink + jnp.sum(
                    shares, axis=1, keepdims=True
                )
                wide_ref[mine, cols] = wide_ref[mine, cols] * shrink + dot(
                    shares.astype(BF16), values
                )
        return carry

    lax.fori_loop(0, me + 1, step_fn, 0)
    for h in range(heads):
        cols = slice(h * dim, (h + 1) * dim)
        total = total_ref[h]
        mixed = wide_ref[:, cols] / total
        wide_ref[:, cols] = mixed
        mixed_ref[:, cols] = mixed.astype(BF16)
        log_ref[:, h : h + 1] = peak_ref[h] + jnp.log(total)


def backward_kernel(
    heads, ctx_ref, starts_ref, table_ref, q_ref, k_ref, v_ref, g_ref, wide_ref, log_ref,
    dq_ref, dk_ref, dv_ref, diag_ref, band_ref, sums_ref, dlogit_ref, share_ref, acc_ref,
):
    rows = q_ref.shape[0]
    span = 2 * rows
    dim = q_ref.shape[1] // heads
    me = ctx_ref[0]
    dk_ref[...] = jnp.zeros_like(dk_ref)
    dv_ref[...] = jnp.zeros_like(dv_ref)
    diag_ref[...] = jnp.zeros_like(diag_ref)
    acc_ref[...] = jnp.zeros_like(acc_ref)

    def step_fn(step, carry):
        delta = me - step
        bias_band(delta, rows, heads, starts_ref, table_ref, band_ref)
        at = pl.multiple_of(step * rows, rows)
        for h in range(heads):
            cols = slice(h * dim, (h + 1) * dim)
            keys = k_ref[pl.ds(at, rows), cols]
            values = v_ref[pl.ds(at, rows), cols]
            sums_ref[...] = jnp.zeros_like(sums_ref)
            for a in range(rows // SUB):
                mine = slice(a * SUB, (a + 1) * SUB)
                off = rows - SUB - SUB * a
                query = q_ref[mine, cols] * BF16(dim ** -0.5)
                grad = g_ref[mine, cols]
                inner = jnp.sum(grad.astype(F32) * wide_ref[mine, cols], axis=1, keepdims=True)
                logits = dot(query, keys, 1, 1) + band_ref[h, :, off : off + rows]
                shares = jnp.exp(logits - log_ref[mine, h : h + 1])
                dlogits = shares * (dot(grad, values, 1, 1) - inner)
                sums_ref[:, off : off + rows] += dlogits
                low = dlogits.astype(BF16)
                share_ref[mine, :] = shares.astype(BF16)
                dlogit_ref[mine, :] = low
                acc_ref[mine, cols] += dot(low, keys)
            dk_ref[pl.ds(at, rows), cols] = (
                dot(dlogit_ref[...], q_ref[:, cols], 0, 0) * dim ** -0.5
            ).astype(BF16)
            dv_ref[pl.ds(at, rows), cols] = dot(share_ref[...], g_ref[:, cols], 0, 0).astype(BF16)
            folded = sums_ref[...]
            width = SUB // 2
            while width >= 8:
                folded = folded[:width] + pltpu.roll(folded[width:], span - width, 1)
                width //= 2
            diag_ref[h, delta] = folded
        return carry

    lax.fori_loop(0, me + 1, step_fn, 0)
    dq_ref[...] = (acc_ref[...] * dim ** -0.5).astype(BF16)


def specs(*kinds):
    return [pl.BlockSpec(memory_space=pltpu.SMEM if k == "s" else pltpu.VMEM) for k in kinds]


def attend_forward(me, starts, table, query, keys, values):
    rows, width = query.shape
    heads = table.shape[1]
    return pl.pallas_call(
        functools.partial(forward_kernel, heads),
        out_shape=(
            jax.ShapeDtypeStruct((rows, width), BF16),
            jax.ShapeDtypeStruct((rows, width), F32),
            jax.ShapeDtypeStruct((rows, heads), F32),
        ),
        in_specs=specs(*"sssvvv"),
        out_specs=tuple(specs(*"vvv")),
        scratch_shapes=[
            pltpu.VMEM((heads, SUB, 2 * rows), F32),
            pltpu.VMEM((heads, rows, 1), F32),
            pltpu.VMEM((heads, rows, 1), F32),
        ],
        compiler_params=pltpu.CompilerParams(vmem_limit_bytes=40 * 2**20),
        name="attend_forward",
    )(me, starts, table, query, keys, values)


def attend_backward(me, starts, table, query, keys, values, grad, wide, logs):
    rows, width = query.shape
    length = keys.shape[0]
    heads = table.shape[1]
    return pl.pallas_call(
        functools.partial(backward_kernel, heads),
        out_shape=(
            jax.ShapeDtypeStruct((rows, width), BF16),
            jax.ShapeDtypeStruct((length, width), BF16),
            jax.ShapeDtypeStruct((length, width), BF16),
            jax.ShapeDtypeStruct((heads, length // rows, 8, 2 * rows), F32),
        ),
        in_specs=specs(*"sssvvvvvv"),
        out_specs=tuple(specs(*"vvvv")),
        scratch_shapes=[
            pltpu.VMEM((heads, SUB, 2 * rows), F32),
            pltpu.VMEM((SUB, 2 * rows), F32),
            pltpu.VMEM((rows, rows), BF16),
            pltpu.VMEM((rows, rows), BF16),
            pltpu.VMEM((rows, width), F32),
        ],
        compiler_params=pltpu.CompilerParams(vmem_limit_bytes=40 * 2**20),
        name="attend_backward",
    )(me, starts, table, query, keys, values, grad, wide, logs)


def tensor_peers():
    mine = lax.axis_index("tensor")
    pair = mine + 1 - 2 * lax.rem(mine, 2)
    return mine, pair, lax.rem(mine + 2, 4), lax.rem(pair + 2, 4)


def remote(src, dst, send, recv, to):
    return pltpu.make_async_remote_copy(
        src_ref=src, dst_ref=dst, send_sem=send, recv_sem=recv,
        device_id=to, device_id_type=pl.DeviceIdType.MESH,
    )


def meet(targets):
    barrier = pltpu.get_barrier_semaphore()
    for to in targets:
        pl.semaphore_signal(barrier, inc=1, device_id=to, device_id_type=pl.DeviceIdType.MESH)
    pl.semaphore_wait(barrier, len(targets))


def group_target(index, ctxs):
    return {"dp": index // ctxs, "ctx": lax.rem(index, ctxs)}


def gather_kernel(x_ref, out_ref, send, recv):
    mine, pair, across, _ = tensor_peers()
    meet([{"tensor": pair}, {"tensor": across}])
    far = remote(x_ref, out_ref.at[mine], send.at[0], recv.at[0], {"tensor": across})
    near = remote(x_ref, out_ref.at[mine], send.at[1], recv.at[1], {"tensor": pair})
    far.start()
    near.start()
    out_ref[mine] = x_ref[...]
    far.wait_recv()
    relay = remote(
        out_ref.at[across], out_ref.at[across], send.at[2], recv.at[2], {"tensor": pair}
    )
    relay.start()
    near.wait_recv()
    relay.wait_recv()
    far.wait_send()
    near.wait_send()
    relay.wait_send()


def tensor_gather(x, ident):
    rows, width = x.shape
    out = pl.pallas_call(
        gather_kernel,
        out_shape=jax.ShapeDtypeStruct((4, rows, width), x.dtype),
        in_specs=specs("v"),
        out_specs=specs("v")[0],
        scratch_shapes=[pltpu.SemaphoreType.DMA((3,)), pltpu.SemaphoreType.DMA((3,))],
        compiler_params=pltpu.CompilerParams(
            collective_id=ident, has_side_effects=True, vmem_limit_bytes=32 * 2**20
        ),
        name="tensor_gather",
    )(x)
    return out.reshape(4 * rows, width)


def scatter_kernel(x_ref, out_ref, got, half, crossed, send, recv):
    mine, pair, across, diagonal = tensor_peers()
    meet([{"tensor": pair}, {"tensor": across}])
    first = remote(x_ref.at[diagonal], got.at[0], send.at[0], recv.at[0], {"tensor": pair})
    second = remote(x_ref.at[pair], got.at[1], send.at[1], recv.at[1], {"tensor": pair})
    first.start()
    second.start()
    first.wait_recv()
    half[...] = (x_ref[across].astype(F32) + got[0].astype(F32)).astype(BF16)
    third = remote(half, crossed, send.at[2], recv.at[2], {"tensor": across})
    third.start()
    second.wait_recv()
    out_ref[...] = x_ref[mine].astype(F32) + got[1].astype(F32)
    third.wait_recv()
    out_ref[...] += crossed[...].astype(F32)
    first.wait_send()
    second.wait_send()
    third.wait_send()


def tensor_scatter(x, ident):
    rows, width = x.shape
    part = rows // 4
    return pl.pallas_call(
        scatter_kernel,
        out_shape=jax.ShapeDtypeStruct((part, width), F32),
        in_specs=specs("v"),
        out_specs=specs("v")[0],
        scratch_shapes=[
            pltpu.VMEM((2, part, width), BF16),
            pltpu.VMEM((part, width), BF16),
            pltpu.VMEM((part, width), BF16),
            pltpu.SemaphoreType.DMA((3,)),
            pltpu.SemaphoreType.DMA((3,)),
        ],
        compiler_params=pltpu.CompilerParams(
            collective_id=ident, has_side_effects=True, vmem_limit_bytes=32 * 2**20
        ),
        name="tensor_scatter",
    )(x.astype(BF16).reshape(4, part, width))


def group_meet(me, groups, ctxs, pair, across):
    barrier = pltpu.get_barrier_semaphore()
    for to in (pair, across):
        pl.semaphore_signal(
            barrier, inc=1, device_id={"tensor": to}, device_id_type=pl.DeviceIdType.MESH
        )

    def greet(k, carry):
        pl.semaphore_signal(
            barrier, inc=1, device_id=group_target(lax.rem(me + k, groups), ctxs),
            device_id_type=pl.DeviceIdType.MESH,
        )
        return carry

    lax.fori_loop(1, groups, greet, 0)
    pl.semaphore_wait(barrier, groups + 1)


def dispatch_kernel(ctxs, x_ref, out_ref, send, recv, far_send, far_recv, near_send, near_recv,
                    relay_send, relay_recv):
    groups = x_ref.shape[0]
    mine, pair, across, _ = tensor_peers()
    me = lax.axis_index("dp") * ctxs + lax.axis_index("ctx")
    group_meet(me, groups, ctxs, pair, across)

    def shipment(k):
        to = lax.rem(me + k, groups)
        return remote(x_ref.at[to], out_ref.at[mine, me], send.at[k], recv.at[k],
                      group_target(to, ctxs))

    def far(k, g):
        return remote(out_ref.at[mine, g], out_ref.at[mine, g], far_send.at[k], far_recv.at[k],
                      {"tensor": across})

    def near(k, g):
        return remote(out_ref.at[mine, g], out_ref.at[mine, g], near_send.at[k],
                      near_recv.at[k], {"tensor": pair})

    def relay(k, g):
        return remote(out_ref.at[across, g], out_ref.at[across, g], relay_send.at[k],
                      relay_recv.at[k], {"tensor": pair})

    def ship(k, carry):
        shipment(k).start()
        return carry

    lax.fori_loop(1, groups, ship, 0)
    out_ref[mine, me] = x_ref[me]
    far(0, me).start()
    near(0, me).start()

    def forward(k, carry):
        shipment(k).wait_recv()
        g = lax.rem(me + groups - k, groups)
        far(k, g).start()
        near(k, g).start()
        past = lax.rem(me + groups - k + 1, groups)
        far(k - 1, past).wait_recv()
        relay(k - 1, past).start()
        return carry

    lax.fori_loop(1, groups, forward, 0)
    last = lax.rem(me + 1, groups)
    far(groups - 1, last).wait_recv()
    relay(groups - 1, last).start()

    def finish(k, carry):
        g = lax.rem(me + groups - k, groups)
        near(k, g).wait_recv()
        relay(k, g).wait_recv()
        far(k, g).wait_send()
        near(k, g).wait_send()
        relay(k, g).wait_send()
        return carry

    lax.fori_loop(0, groups, finish, 0)

    def sent(k, carry):
        shipment(k).wait_send()
        return carry

    lax.fori_loop(1, groups, sent, 0)


def dispatch(x, ctxs, ident):
    groups, rows, width = x.shape
    sems = [pltpu.SemaphoreType.DMA((groups,))] * 8
    return pl.pallas_call(
        functools.partial(dispatch_kernel, ctxs),
        out_shape=jax.ShapeDtypeStruct((4, groups, rows, width), x.dtype),
        in_specs=specs("v"),
        out_specs=specs("v")[0],
        scratch_shapes=sems,
        compiler_params=pltpu.CompilerParams(
            collective_id=ident, has_side_effects=True, vmem_limit_bytes=40 * 2**20
        ),
        name="dispatch",
    )(x)


def combine_kernel(ctxs, x_ref, out_ref, got, half, crossed, total,
                   near_send, near_recv, far_send, far_recv, send, recv):
    groups = x_ref.shape[1]
    mine, pair, across, diagonal = tensor_peers()
    me = lax.axis_index("dp") * ctxs + lax.axis_index("ctx")
    group_meet(me, groups, ctxs, pair, across)

    def near(k, g, which, block):
        return remote(x_ref.at[block, g], got.at[which, k], near_send.at[which, k],
                      near_recv.at[which, k], {"tensor": pair})

    def far(k):
        return remote(half.at[k], crossed.at[k], far_send.at[k], far_recv.at[k],
                      {"tensor": across})

    def shipment(k):
        return remote(total.at[k], out_ref.at[me], send.at[k], recv.at[k],
                      group_target(lax.rem(me + k, groups), ctxs))

    def begin(k, carry):
        g = lax.rem(me + k, groups)
        near(k, g, 0, diagonal).start()
        near(k, g, 1, pair).start()
        return carry

    lax.fori_loop(0, groups, begin, 0)

    def cross(k, carry):
        g = lax.rem(me + k, groups)
        near(k, g, 0, diagonal).wait_recv()
        half[k] = (x_ref[across, g].astype(F32) + got[0, k].astype(F32)).astype(BF16)
        far(k).start()
        return carry

    lax.fori_loop(0, groups, cross, 0)

    def add(k):
        g = lax.rem(me + k, groups)
        near(k, g, 1, pair).wait_recv()
        far(k).wait_recv()
        return (
            x_ref[mine, g].astype(F32) + got[1, k].astype(F32) + crossed[k].astype(F32)
        ).astype(BF16)

    def ship(k, carry):
        total[k] = add(k)
        shipment(k).start()
        return carry

    out_ref[me] = add(0)
    lax.fori_loop(1, groups, ship, 0)

    def finish(k, carry):
        g = lax.rem(me + k, groups)
        near(k, g, 0, diagonal).wait_send()
        near(k, g, 1, pair).wait_send()
        far(k).wait_send()
        return carry

    lax.fori_loop(0, groups, finish, 0)

    def land(k, carry):
        shipment(k).wait_recv()
        shipment(k).wait_send()
        return carry

    lax.fori_loop(1, groups, land, 0)


def combine(x, ctxs, ident):
    _, groups, rows, width = x.shape
    block = (groups, rows, width)
    one = pltpu.SemaphoreType.DMA((groups,))
    two = pltpu.SemaphoreType.DMA((2, groups))
    return pl.pallas_call(
        functools.partial(combine_kernel, ctxs),
        out_shape=jax.ShapeDtypeStruct(block, BF16),
        in_specs=specs("v"),
        out_specs=specs("v")[0],
        scratch_shapes=[
            pltpu.VMEM((2,) + block, BF16),
            pltpu.VMEM(block, BF16),
            pltpu.VMEM(block, BF16),
            pltpu.VMEM(block, BF16),
            two, two, one, one, one, one,
        ],
        compiler_params=pltpu.CompilerParams(
            collective_id=ident, has_side_effects=True, vmem_limit_bytes=52 * 2**20
        ),
        name="combine",
    )(x)


def all_meet(me, groups, ctxs, mine):
    barrier = pltpu.get_barrier_semaphore()

    def greet(k, carry):
        pl.semaphore_signal(
            barrier, inc=1, device_id=group_target(lax.rem(me + k, groups), ctxs),
            device_id_type=pl.DeviceIdType.MESH,
        )
        return carry

    lax.fori_loop(1, groups, greet, 0)
    for k in range(1, 4):
        pl.semaphore_signal(
            barrier, inc=1, device_id={"tensor": lax.rem(mine + k, 4)},
            device_id_type=pl.DeviceIdType.MESH,
        )
    pl.semaphore_wait(barrier, groups + 2)


def spread(out_ref, dps, ctxs, send, recv, side_send, side_recv):
    at_dp, at_ctx = lax.axis_index("dp"), lax.axis_index("ctx")

    def along(k):
        block = out_ref.at[at_dp * ctxs + at_ctx]
        return remote(block, block, send.at[k], recv.at[k], {"dp": lax.rem(at_dp + k, dps)})

    def side(k, c):
        block = out_ref.at[lax.rem(at_dp + dps - k, dps) * ctxs + at_ctx]
        return remote(block, block, side_send.at[k, c], side_recv.at[k, c],
                      {"ctx": lax.rem(at_ctx + c, ctxs)})

    for k in range(1, dps):
        along(k).start()
    for k in range(dps):
        if k:
            along(k).wait_recv()
        for c in range(1, ctxs):
            side(k, c).start()
    for k in range(dps):
        for c in range(1, ctxs):
            side(k, c).wait_recv()
            side(k, c).wait_send()
        if k:
            along(k).wait_send()


def spread_sems(dps, ctxs):
    line, plane = pltpu.SemaphoreType.DMA((dps,)), pltpu.SemaphoreType.DMA((dps, ctxs))
    return [line, line, plane, plane]


def group_gather_kernel(dps, ctxs, x_ref, out_ref, *sems):
    me = lax.axis_index("dp") * ctxs + lax.axis_index("ctx")
    all_meet(me, dps * ctxs, ctxs, lax.axis_index("tensor"))
    out_ref[me] = x_ref[...]
    spread(out_ref, dps, ctxs, *sems)


def group_gather(x, dps, ctxs, ident):
    rows, width = x.shape
    out = pl.pallas_call(
        functools.partial(group_gather_kernel, dps, ctxs),
        out_shape=jax.ShapeDtypeStruct((dps * ctxs, rows, width), x.dtype),
        in_specs=specs("v"),
        out_specs=specs("v")[0],
        scratch_shapes=spread_sems(dps, ctxs),
        compiler_params=pltpu.CompilerParams(
            collective_id=ident, has_side_effects=True, vmem_limit_bytes=32 * 2**20
        ),
        name="group_gather",
    )(x)
    return out.reshape(dps * ctxs * rows, width)


def group_sum_kernel(dps, ctxs, w_ref, s_ref, out_ref, small_ref, got, across, near, far,
                     send, recv, t_send, t_recv, s_send, s_recv, *sems):
    groups = dps * ctxs
    me = lax.axis_index("dp") * ctxs + lax.axis_index("ctx")
    mine = lax.axis_index("tensor")
    all_meet(me, groups, ctxs, mine)

    def small(k):
        return remote(s_ref, across.at[k], t_send.at[k], t_recv.at[k],
                      {"tensor": lax.rem(mine + k, 4)})

    def block(k):
        to = lax.rem(me + k, groups)
        return remote(w_ref.at[to], got.at[k], send.at[k], recv.at[k], group_target(to, ctxs))

    def tiny(k):
        return remote(near, far.at[k], s_send.at[k], s_recv.at[k],
                      group_target(lax.rem(me + k, groups), ctxs))

    def start_tiny(k, carry):
        tiny(k).start()
        return carry

    def start_block(k, carry):
        block(k).start()
        return carry

    for k in range(1, 4):
        small(k).start()
    lax.fori_loop(1, groups, start_block, 0)
    total = s_ref[...].astype(F32)
    for k in range(1, 4):
        small(k).wait_recv()
        total = total + across[k].astype(F32)
    near[...] = total.astype(BF16)
    lax.fori_loop(1, groups, start_tiny, 0)

    def add(k, acc):
        block(k).wait_recv()
        return acc + got[k].astype(F32)

    out_ref[me] = lax.fori_loop(1, groups, add, w_ref[me].astype(F32)).astype(BF16)
    spread(out_ref, dps, ctxs, *sems)

    def add_tiny(k, acc):
        tiny(k).wait_recv()
        return acc + far[k].astype(F32)

    small_ref[...] = lax.fori_loop(1, groups, add_tiny, near[...].astype(F32))

    def leave(k, carry):
        block(k).wait_send()
        tiny(k).wait_send()
        return carry

    lax.fori_loop(1, groups, leave, 0)
    for k in range(1, 4):
        small(k).wait_send()


def group_sum(grads, small, dps, ctxs, ident):
    groups = dps * ctxs
    rows, width = grads.shape
    block = (groups, rows // groups, width)
    line = pltpu.SemaphoreType.DMA((groups,))
    four = pltpu.SemaphoreType.DMA((4,))
    out, total = pl.pallas_call(
        functools.partial(group_sum_kernel, dps, ctxs),
        out_shape=(
            jax.ShapeDtypeStruct(block, BF16), jax.ShapeDtypeStruct(small.shape, F32),
        ),
        in_specs=specs("v", "v"),
        out_specs=tuple(specs("v", "v")),
        scratch_shapes=[
            pltpu.VMEM(block, BF16),
            pltpu.VMEM((4,) + small.shape, BF16),
            pltpu.VMEM(small.shape, BF16),
            pltpu.VMEM((groups,) + small.shape, BF16),
            line, line, four, four, line, line,
        ] + spread_sems(dps, ctxs),
        compiler_params=pltpu.CompilerParams(
            collective_id=ident, has_side_effects=True, vmem_limit_bytes=48 * 2**20
        ),
        name="group_sum",
    )(grads.astype(BF16).reshape(block), small)
    return out.reshape(rows, width).astype(F32), total


def halve(x):
    width = x.shape[-1] // 2
    return jnp.concatenate([x[..., :width], x[..., width:]], axis=-2)


def unhalve(x):
    rows = x.shape[-2] // 2
    return jnp.concatenate([x[..., :rows, :], x[..., rows:, :]], axis=-1)


def table_grad(diag, starts):
    heads, blocks, sub, span = diag.shape
    delta = lax.broadcasted_iota(jnp.int32, (blocks, sub, span), 0)
    row = lax.broadcasted_iota(jnp.int32, (blocks, sub, span), 1)
    lane = lax.broadcasted_iota(jnp.int32, (blocks, sub, span), 2)
    far = lane_distance(delta, span // 2, lane) + row
    later = jnp.concatenate([starts[1:], jnp.full((1,), 2**30, jnp.int32)])
    inside = (far[None] >= starts[:, None, None, None]) & (far[None] < later[:, None, None, None])
    return jnp.sum(
        jnp.where(inside[:, None], diag[None], 0.0), axis=(2, 3, 4)
    )


def hi_lo(x):
    hi = x.astype(BF16)
    return hi, (x - hi.astype(F32)).astype(BF16)


def norm_scale(value):
    return lax.rsqrt(jnp.mean(value * value, axis=-1, keepdims=True) + EPS)


def norm_backward(value, scale, gain, grad_normed):
    scaled = grad_normed * gain
    grad_value = scale * scaled - value * scale**3 * jnp.mean(
        value * scaled, axis=-1, keepdims=True
    )
    return grad_value, jnp.sum(grad_normed * value * scale, axis=0)


def on_device(
    inputs, gain_attention, w_query, w_key, w_value, w_output, bias_table, bucket_start,
    gain_experts, w_router, w_up, w_down, expert_ids, slot_index, cotangent,
):
    sequences, rows, width = inputs.shape
    tokens = sequences * rows
    experts = w_router.shape[1]
    top = expert_ids.shape[2]
    capacity = 5 * tokens * top // (4 * experts)
    heads = bias_table.shape[1]
    split = lax.axis_size("tensor")
    ctxs = lax.axis_size("ctx")
    dps = lax.axis_size("dp")
    at_tensor = lax.axis_index("tensor")
    at_ctx = lax.axis_index("ctx")
    me = at_ctx.astype(jnp.int32).reshape(1)
    part = tokens // split
    slots = (capacity // split + 7) // 8 * 8
    own = capacity // split
    shard_rows = experts * slots
    groups = ("dp", "ctx")

    def my_tokens(x):
        return lax.dynamic_slice_in_dim(x, at_tensor * part, part, 0)

    def exchange(x):
        group = lax.axis_index("dp") * ctxs + at_ctx
        blocks = x.reshape((experts, slots) + x.shape[1:])
        got = [lax.dynamic_index_in_dim(blocks, group, 0)]
        for k in range(1, experts):
            moves = [(i, (i + k) % experts) for i in range(experts)]
            block = lax.dynamic_index_in_dim(blocks, lax.rem(group + k, experts), 0)
            got.append(lax.ppermute(block, groups, moves))
        behind = jnp.concatenate(got[::-1], axis=0)
        twice = jnp.concatenate([behind, behind], axis=0)
        return lax.dynamic_slice_in_dim(twice, experts - 1 - group, experts, 0)

    route = expert_ids.reshape(tokens, top)
    place = slot_index.reshape(tokens, top)
    local = place - at_tensor * own
    inside = (place >= 0) & (local >= 0) & (local < own)
    row_of = jnp.where(inside, route * slots + local, -1)
    spots = jnp.arange(shard_rows, dtype=jnp.int32)
    hits = [row_of[:, k : k + 1] == spots[None, :] for k in range(top)]
    ones = [h.astype(BF16) for h in hits]
    any_hit = sum(ones[1:], ones[0])
    cot = cotangent.reshape(tokens, width)

    hh = w_query.shape[1]
    all_w = group_gather(
        jnp.concatenate([w_query, w_key, w_value, w_output], axis=1), dps, ctxs, 8
    )
    qkv_w, output_w = all_w[:, : 3 * hh], all_w[:, 3 * hh :]
    cot_rows = lax.all_gather(
        exchange(dot(any_hit, cot, 0, 0).astype(BF16)), "tensor", axis=0
    ).reshape(split * shard_rows, width)
    source = inputs.astype(F32).reshape(tokens, width)
    scale_one = norm_scale(source)
    normed_one = (source * scale_one * gain_attention).astype(BF16)
    qkv = dot(normed_one, qkv_w).astype(BF16).reshape(sequences, rows, 3 * hh)
    kv_all = lax.all_gather(qkv[:, :, hh:], "ctx", axis=1, tiled=True)
    seen = [
        attend_forward(
            me, bucket_start, bias_table,
            qkv[b, :, :hh], kv_all[b, :, :hh], kv_all[b, :, hh:],
        )
        for b in range(sequences)
    ]
    mixed = jnp.concatenate([s[0] for s in seen], axis=0)
    source_mine = my_tokens(source)
    hidden = source_mine + tensor_scatter(dot(mixed, output_w, 1, 1), 0)
    scale_two = norm_scale(hidden)
    normed_mine = (hidden * scale_two * gain_experts).astype(BF16)
    normed_two = tensor_gather(normed_mine, 1)

    router_logits = dot(normed_two, w_router)
    picks = route[:, :, None] == jnp.arange(experts, dtype=jnp.int32)[None, None, :]
    chosen = jnp.sum(jnp.where(picks, router_logits[:, None, :], 0.0), axis=-1)
    gates = jax.nn.softmax(chosen, axis=-1)
    row_gate = sum(
        jnp.sum(jnp.where(hits[k], gates[:, k : k + 1], 0.0), axis=0) for k in range(top)
    )

    hi_and_lo = jnp.stack(hi_lo(row_gate.reshape(experts, slots)), axis=1)
    gate_block = jnp.pad(hi_and_lo, ((0, 0), (0, 14), (0, width // 2 - slots)))
    rows_out = dot(any_hit, normed_two, 0, 0).astype(BF16).reshape(experts, slots, width)
    arrived = dispatch(jnp.concatenate([halve(rows_out), gate_block], axis=1), ctxs, 2)
    buffer = unhalve(arrived[:, :, : 2 * slots]).reshape(split * shard_rows, width)
    gate_rows = (
        arrived[:, :, 2 * slots, :slots].astype(F32)
        + arrived[:, :, 2 * slots + 1, :slots].astype(F32)
    ).reshape(split * shard_rows, 1)
    grad_produced = (gate_rows * cot_rows.astype(F32)).astype(BF16)
    up, down = w_up[0], w_down[0]
    before = dot(buffer, up)
    activated, gelu_pullback = jax.vjp(jax.nn.gelu, before)
    activated = activated.astype(BF16)
    partial_out = dot(activated, down).astype(BF16)
    grad_before = gelu_pullback(dot(grad_produced, down, 1, 1))[0].astype(BF16)
    partial_grad = dot(grad_before, up, 1, 1).astype(BF16)
    shares = (split, experts, slots, width)
    came_back = combine(
        jnp.concatenate(
            [halve(partial_out.reshape(shares)), halve(partial_grad.reshape(shares))], axis=2
        ),
        ctxs, 3,
    )
    returned = unhalve(came_back[:, : 2 * slots]).reshape(shard_rows, width)
    grad_returned = unhalve(came_back[:, 2 * slots :]).reshape(shard_rows, width)
    grad_down = dot(activated, grad_produced, 0, 0)
    grad_up = dot(buffer, grad_before, 0, 0)

    cot32 = cot.astype(F32)
    picked = [dot(one, returned) for one in ones]
    mixture = sum(gates[:, k : k + 1] * picked[k] for k in range(top))
    gate_part = jnp.stack([jnp.sum(cot32 * picked[k], axis=-1) for k in range(top)], axis=1)
    part_hi, part_lo = hi_lo(gate_part)
    summed = tensor_scatter(
        jnp.concatenate(
            [
                mixture.astype(BF16),
                dot(any_hit, grad_returned).astype(BF16),
                jnp.pad(jnp.concatenate([part_hi, part_lo], axis=1), ((0, 0), (0, 128 - 2 * top))),
            ],
            axis=1,
        ),
        4,
    )
    result = hidden + summed[:, :width]
    layer_out = lax.all_gather(result.astype(BF16), "tensor", axis=0, tiled=True)
    grad_gates = (
        summed[:, 2 * width : 2 * width + top] + summed[:, 2 * width + top : 2 * width + 2 * top]
    )
    gates_mine = my_tokens(gates)
    grad_chosen = gates_mine * (
        grad_gates - jnp.sum(gates_mine * grad_gates, axis=-1, keepdims=True)
    )
    grad_logits = jnp.sum(
        jnp.where(my_tokens(picks), grad_chosen[:, :, None], 0.0), axis=1
    ).astype(BF16)
    grad_router = dot(normed_mine, grad_logits, 0, 0)
    grad_normed_two = summed[:, width : 2 * width] + dot(grad_logits, w_router, 1, 1)
    grad_back, grad_gain_two = norm_backward(hidden, scale_two, gain_experts, grad_normed_two)
    grad_hidden = my_tokens(cot).astype(F32) + grad_back
    grad_branch = tensor_gather(grad_hidden.astype(BF16), 5)

    grad_mixed = dot(grad_branch, output_w).astype(BF16).reshape(sequences, rows, hh)
    grad_output = dot(grad_branch, mixed, 0, 0)
    back = [
        attend_backward(
            me, bucket_start, bias_table,
            qkv[b, :, :hh], kv_all[b, :, :hh], kv_all[b, :, hh:],
            grad_mixed[b], seen[b][1], seen[b][2],
        )
        for b in range(sequences)
    ]
    kv_part = jnp.stack([jnp.concatenate([b[1], b[2]], axis=1) for b in back])
    kv_grad = lax.psum_scatter(kv_part, "ctx", scatter_dimension=1, tiled=True)
    qkv_grad = jnp.concatenate([jnp.stack([b[0] for b in back]), kv_grad], axis=2).reshape(
        tokens, 3 * hh
    )
    grad_table = sum(table_grad(b[3], bucket_start) for b in back)
    grad_normed_one = tensor_scatter(dot(qkv_grad, qkv_w, 1, 1), 6)
    grad_back_one, grad_gain_one = norm_backward(
        source_mine, my_tokens(scale_one), gain_attention, grad_normed_one
    )
    grad_inputs = tensor_gather((grad_hidden + grad_back_one).astype(BF16), 7).astype(F32)

    flat_table = jnp.pad(
        grad_table.reshape(1, -1), ((0, 0), (0, width - grad_table.size))
    )
    flat_table = jnp.roll(flat_table, at_tensor * grad_table.size, axis=1)
    rows_small = jnp.concatenate(
        [grad_gain_one[None], grad_gain_two[None], grad_router.T, flat_table], axis=0
    ).astype(BF16)
    rows_small = jnp.pad(rows_small, ((0, -rows_small.shape[0] % 16), (0, 0)))
    grads, small = group_sum(
        jnp.concatenate([dot(normed_one, qkv_grad, 0, 0), grad_output], axis=1),
        rows_small, dps, ctxs, 9,
    )
    grad_table = lax.dynamic_slice_in_dim(
        small[2 + experts], at_tensor * grad_table.size, grad_table.size, 0
    ).reshape(grad_table.shape)
    return (
        layer_out.reshape(sequences, rows, width),
        grad_inputs.reshape(sequences, rows, width),
        small[0],
        grads[:, :hh],
        grads[:, hh : 2 * hh],
        grads[:, 2 * hh : 3 * hh],
        grads[:, 3 * hh :],
        grad_table,
        small[1],
        small[2 : 2 + experts].T,
        grad_up[None],
        grad_down[None],
    )


def solution(mesh):
    in_specs = (
        P("dp", "ctx", None),
        P(),
        P(("dp", "ctx"), "tensor"),
        P(("dp", "ctx"), "tensor"),
        P(("dp", "ctx"), "tensor"),
        P(("dp", "ctx"), "tensor"),
        P(None, "tensor"),
        P(),
        P(),
        P(),
        P(("dp", "ctx"), None, "tensor"),
        P(("dp", "ctx"), "tensor", None),
        P("dp", "ctx", None),
        P("dp", "ctx", None),
        P("dp", "ctx", None),
    )
    out_specs = (
        P("dp", "ctx", None),
        P("dp", "ctx", None),
        P(),
        P(None, "tensor"),
        P(None, "tensor"),
        P(None, "tensor"),
        P(None, "tensor"),
        P(None, "tensor"),
        P(),
        P(),
        P(("dp", "ctx"), None, "tensor"),
        P(("dp", "ctx"), "tensor", None),
    )
    return jax.shard_map(
        on_device, mesh=mesh, in_specs=in_specs, out_specs=out_specs, check_vma=False
    )
```

```python
import functools

import jax
import jax.numpy as jnp
from jax import lax
from jax.experimental import pallas as pl
from jax.experimental.pallas import tpu as pltpu
from jax.sharding import PartitionSpec as P

EPS = 1e-06
MASKED = -1e30
SUB = 128
F32 = jnp.float32
BF16 = jnp.bfloat16


def dot(a, b, ca=1, cb=0):
    return lax.dot_general(a, b, (((ca,), (cb,)), ((), ())), preferred_element_type=F32)


def lane_distance(delta, rows, v):
    span = 2 * rows
    v = jnp.where(v > span - SUB, v - span, v)
    return delta * rows + rows - SUB - v


def bias_band(delta, rows, heads, starts_ref, table_ref, band_ref):
    span = 2 * rows
    far = lane_distance(delta, rows, lax.broadcasted_iota(jnp.int32, (8, span), 1))
    lines = [jnp.full((8, span), MASKED, F32) for _ in range(heads)]
    for b in range(table_ref.shape[0]):
        reached = far >= starts_ref[b]
        for h in range(heads):
            lines[h] = jnp.where(reached, table_ref[b, h], lines[h])
    for h in range(heads):
        wide = jnp.broadcast_to(lines[h][0:1], (SUB, span))
        band_ref[h] = pltpu.roll(wide, 0, 1, stride=1, stride_axis=0)


def forward_kernel(
    heads, ctx_ref, starts_ref, table_ref, q_ref, k_ref, v_ref,
    mixed_ref, wide_ref, log_ref, band_ref, peak_ref, total_ref,
):
    rows = q_ref.shape[0]
    dim = q_ref.shape[1] // heads
    me = ctx_ref[0]
    peak_ref[...] = jnp.full_like(peak_ref, MASKED)
    total_ref[...] = jnp.zeros_like(total_ref)
    wide_ref[...] = jnp.zeros_like(wide_ref)

    def step_fn(step, carry):
        bias_band(me - step, rows, heads, starts_ref, table_ref, band_ref)
        at = pl.multiple_of(step * rows, rows)
        for h in range(heads):
            cols = slice(h * dim, (h + 1) * dim)
            keys = k_ref[pl.ds(at, rows), cols]
            values = v_ref[pl.ds(at, rows), cols]
            for a in range(rows // SUB):
                mine = slice(a * SUB, (a + 1) * SUB)
                off = rows - SUB - SUB * a
                query = q_ref[mine, cols] * BF16(dim ** -0.5)
                logits = dot(query, keys, 1, 1) + band_ref[h, :, off : off + rows]
                old = peak_ref[h, mine, :]
                new = jnp.maximum(old, jnp.max(logits, axis=1, keepdims=True))
                shares = jnp.exp(logits - new)
                shrink = jnp.exp(old - new)
                peak_ref[h, mine, :] = new
                total_ref[h, mine, :] = total_ref[h, mine, :] * shrink + jnp.sum(
                    shares, axis=1, keepdims=True
                )
                wide_ref[mine, cols] = wide_ref[mine, cols] * shrink + dot(
                    shares.astype(BF16), values
                )
        return carry

    lax.fori_loop(0, me + 1, step_fn, 0)
    for h in range(heads):
        cols = slice(h * dim, (h + 1) * dim)
        total = total_ref[h]
        mixed = wide_ref[:, cols] / total
        wide_ref[:, cols] = mixed
        mixed_ref[:, cols] = mixed.astype(BF16)
        log_ref[:, h : h + 1] = peak_ref[h] + jnp.log(total)


def backward_kernel(
    heads, ctx_ref, starts_ref, table_ref, q_ref, k_ref, v_ref, g_ref, wide_ref, log_ref,
    dq_ref, dk_ref, dv_ref, diag_ref, band_ref, sums_ref, dlogit_ref, share_ref, acc_ref,
):
    rows = q_ref.shape[0]
    span = 2 * rows
    dim = q_ref.shape[1] // heads
    me = ctx_ref[0]
    dk_ref[...] = jnp.zeros_like(dk_ref)
    dv_ref[...] = jnp.zeros_like(dv_ref)
    diag_ref[...] = jnp.zeros_like(diag_ref)
    acc_ref[...] = jnp.zeros_like(acc_ref)

    def step_fn(step, carry):
        delta = me - step
        bias_band(delta, rows, heads, starts_ref, table_ref, band_ref)
        at = pl.multiple_of(step * rows, rows)
        for h in range(heads):
            cols = slice(h * dim, (h + 1) * dim)
            keys = k_ref[pl.ds(at, rows), cols]
            values = v_ref[pl.ds(at, rows), cols]
            sums_ref[...] = jnp.zeros_like(sums_ref)
            for a in range(rows // SUB):
                mine = slice(a * SUB, (a + 1) * SUB)
                off = rows - SUB - SUB * a
                query = q_ref[mine, cols] * BF16(dim ** -0.5)
                grad = g_ref[mine, cols]
                inner = jnp.sum(grad.astype(F32) * wide_ref[mine, cols], axis=1, keepdims=True)
                logits = dot(query, keys, 1, 1) + band_ref[h, :, off : off + rows]
                shares = jnp.exp(logits - log_ref[mine, h : h + 1])
                dlogits = shares * (dot(grad, values, 1, 1) - inner)
                sums_ref[:, off : off + rows] += dlogits
                low = dlogits.astype(BF16)
                share_ref[mine, :] = shares.astype(BF16)
                dlogit_ref[mine, :] = low
                acc_ref[mine, cols] += dot(low, keys)
            dk_ref[pl.ds(at, rows), cols] = (
                dot(dlogit_ref[...], q_ref[:, cols], 0, 0) * dim ** -0.5
            ).astype(BF16)
            dv_ref[pl.ds(at, rows), cols] = dot(share_ref[...], g_ref[:, cols], 0, 0).astype(BF16)
            folded = sums_ref[...]
            width = SUB // 2
            while width >= 8:
                folded = folded[:width] + pltpu.roll(folded[width:], span - width, 1)
                width //= 2
            diag_ref[h, delta] = folded
        return carry

    lax.fori_loop(0, me + 1, step_fn, 0)
    dq_ref[...] = (acc_ref[...] * dim ** -0.5).astype(BF16)


def specs(*kinds):
    return [pl.BlockSpec(memory_space=pltpu.SMEM if k == "s" else pltpu.VMEM) for k in kinds]


def attend_forward(me, starts, table, query, keys, values):
    rows, width = query.shape
    heads = table.shape[1]
    return pl.pallas_call(
        functools.partial(forward_kernel, heads),
        out_shape=(
            jax.ShapeDtypeStruct((rows, width), BF16),
            jax.ShapeDtypeStruct((rows, width), F32),
            jax.ShapeDtypeStruct((rows, heads), F32),
        ),
        in_specs=specs(*"sssvvv"),
        out_specs=tuple(specs(*"vvv")),
        scratch_shapes=[
            pltpu.VMEM((heads, SUB, 2 * rows), F32),
            pltpu.VMEM((heads, rows, 1), F32),
            pltpu.VMEM((heads, rows, 1), F32),
        ],
        compiler_params=pltpu.CompilerParams(vmem_limit_bytes=40 * 2**20),
        name="attend_forward",
    )(me, starts, table, query, keys, values)


def attend_backward(me, starts, table, query, keys, values, grad, wide, logs):
    rows, width = query.shape
    length = keys.shape[0]
    heads = table.shape[1]
    return pl.pallas_call(
        functools.partial(backward_kernel, heads),
        out_shape=(
            jax.ShapeDtypeStruct((rows, width), BF16),
            jax.ShapeDtypeStruct((length, width), BF16),
            jax.ShapeDtypeStruct((length, width), BF16),
            jax.ShapeDtypeStruct((heads, length // rows, 8, 2 * rows), F32),
        ),
        in_specs=specs(*"sssvvvvvv"),
        out_specs=tuple(specs(*"vvvv")),
        scratch_shapes=[
            pltpu.VMEM((heads, SUB, 2 * rows), F32),
            pltpu.VMEM((SUB, 2 * rows), F32),
            pltpu.VMEM((rows, rows), BF16),
            pltpu.VMEM((rows, rows), BF16),
            pltpu.VMEM((rows, width), F32),
        ],
        compiler_params=pltpu.CompilerParams(vmem_limit_bytes=40 * 2**20),
        name="attend_backward",
    )(me, starts, table, query, keys, values, grad, wide, logs)


def tensor_peers():
    mine = lax.axis_index("tensor")
    pair = mine + 1 - 2 * lax.rem(mine, 2)
    return mine, pair, lax.rem(mine + 2, 4), lax.rem(pair + 2, 4)


def remote(src, dst, send, recv, to):
    return pltpu.make_async_remote_copy(
        src_ref=src, dst_ref=dst, send_sem=send, recv_sem=recv,
        device_id=to, device_id_type=pl.DeviceIdType.MESH,
    )


def meet(targets):
    barrier = pltpu.get_barrier_semaphore()
    for to in targets:
        pl.semaphore_signal(barrier, inc=1, device_id=to, device_id_type=pl.DeviceIdType.MESH)
    pl.semaphore_wait(barrier, len(targets))


def group_target(index, ctxs):
    return {"dp": index // ctxs, "ctx": lax.rem(index, ctxs)}


def gather_kernel(x_ref, out_ref, send, recv):
    mine, pair, across, _ = tensor_peers()
    meet([{"tensor": pair}, {"tensor": across}])
    far = remote(x_ref, out_ref.at[mine], send.at[0], recv.at[0], {"tensor": across})
    near = remote(x_ref, out_ref.at[mine], send.at[1], recv.at[1], {"tensor": pair})
    far.start()
    near.start()
    out_ref[mine] = x_ref[...]
    far.wait_recv()
    relay = remote(
        out_ref.at[across], out_ref.at[across], send.at[2], recv.at[2], {"tensor": pair}
    )
    relay.start()
    near.wait_recv()
    relay.wait_recv()
    far.wait_send()
    near.wait_send()
    relay.wait_send()


def tensor_gather(x, ident):
    rows, width = x.shape
    out = pl.pallas_call(
        gather_kernel,
        out_shape=jax.ShapeDtypeStruct((4, rows, width), x.dtype),
        in_specs=specs("v"),
        out_specs=specs("v")[0],
        scratch_shapes=[pltpu.SemaphoreType.DMA((3,)), pltpu.SemaphoreType.DMA((3,))],
        compiler_params=pltpu.CompilerParams(
            collective_id=ident, has_side_effects=True, vmem_limit_bytes=32 * 2**20
        ),
        name="tensor_gather",
    )(x)
    return out.reshape(4 * rows, width)


def scatter_kernel(x_ref, out_ref, got, half, crossed, send, recv):
    mine, pair, across, diagonal = tensor_peers()
    meet([{"tensor": pair}, {"tensor": across}])
    first = remote(x_ref.at[diagonal], got.at[0], send.at[0], recv.at[0], {"tensor": pair})
    second = remote(x_ref.at[pair], got.at[1], send.at[1], recv.at[1], {"tensor": pair})
    first.start()
    second.start()
    first.wait_recv()
    half[...] = (x_ref[across].astype(F32) + got[0].astype(F32)).astype(BF16)
    third = remote(half, crossed, send.at[2], recv.at[2], {"tensor": across})
    third.start()
    second.wait_recv()
    out_ref[...] = x_ref[mine].astype(F32) + got[1].astype(F32)
    third.wait_recv()
    out_ref[...] += crossed[...].astype(F32)
    first.wait_send()
    second.wait_send()
    third.wait_send()


def tensor_scatter(x, ident):
    rows, width = x.shape
    part = rows // 4
    return pl.pallas_call(
        scatter_kernel,
        out_shape=jax.ShapeDtypeStruct((part, width), F32),
        in_specs=specs("v"),
        out_specs=specs("v")[0],
        scratch_shapes=[
            pltpu.VMEM((2, part, width), BF16),
            pltpu.VMEM((part, width), BF16),
            pltpu.VMEM((part, width), BF16),
            pltpu.SemaphoreType.DMA((3,)),
            pltpu.SemaphoreType.DMA((3,)),
        ],
        compiler_params=pltpu.CompilerParams(
            collective_id=ident, has_side_effects=True, vmem_limit_bytes=32 * 2**20
        ),
        name="tensor_scatter",
    )(x.astype(BF16).reshape(4, part, width))


def group_meet(me, groups, ctxs, pair, across):
    barrier = pltpu.get_barrier_semaphore()
    for to in (pair, across):
        pl.semaphore_signal(
            barrier, inc=1, device_id={"tensor": to}, device_id_type=pl.DeviceIdType.MESH
        )

    def greet(k, carry):
        pl.semaphore_signal(
            barrier, inc=1, device_id=group_target(lax.rem(me + k, groups), ctxs),
            device_id_type=pl.DeviceIdType.MESH,
        )
        return carry

    lax.fori_loop(1, groups, greet, 0)
    pl.semaphore_wait(barrier, groups + 1)


def dispatch_kernel(ctxs, x_ref, out_ref, send, recv, far_send, far_recv, near_send, near_recv,
                    relay_send, relay_recv):
    groups = x_ref.shape[0]
    mine, pair, across, _ = tensor_peers()
    me = lax.axis_index("dp") * ctxs + lax.axis_index("ctx")
    group_meet(me, groups, ctxs, pair, across)

    def shipment(k):
        to = lax.rem(me + k, groups)
        return remote(x_ref.at[to], out_ref.at[mine, me], send.at[k], recv.at[k],
                      group_target(to, ctxs))

    def far(k, g):
        return remote(out_ref.at[mine, g], out_ref.at[mine, g], far_send.at[k], far_recv.at[k],
                      {"tensor": across})

    def near(k, g):
        return remote(out_ref.at[mine, g], out_ref.at[mine, g], near_send.at[k],
                      near_recv.at[k], {"tensor": pair})

    def relay(k, g):
        return remote(out_ref.at[across, g], out_ref.at[across, g], relay_send.at[k],
                      relay_recv.at[k], {"tensor": pair})

    def ship(k, carry):
        shipment(k).start()
        return carry

    lax.fori_loop(1, groups, ship, 0)
    out_ref[mine, me] = x_ref[me]
    far(0, me).start()
    near(0, me).start()

    def forward(k, carry):
        shipment(k).wait_recv()
        g = lax.rem(me + groups - k, groups)
        far(k, g).start()
        near(k, g).start()
        past = lax.rem(me + groups - k + 1, groups)
        far(k - 1, past).wait_recv()
        relay(k - 1, past).start()
        return carry

    lax.fori_loop(1, groups, forward, 0)
    last = lax.rem(me + 1, groups)
    far(groups - 1, last).wait_recv()
    relay(groups - 1, last).start()

    def finish(k, carry):
        g = lax.rem(me + groups - k, groups)
        near(k, g).wait_recv()
        relay(k, g).wait_recv()
        far(k, g).wait_send()
        near(k, g).wait_send()
        relay(k, g).wait_send()
        return carry

    lax.fori_loop(0, groups, finish, 0)

    def sent(k, carry):
        shipment(k).wait_send()
        return carry

    lax.fori_loop(1, groups, sent, 0)


def dispatch(x, ctxs, ident):
    groups, rows, width = x.shape
    sems = [pltpu.SemaphoreType.DMA((groups,))] * 8
    return pl.pallas_call(
        functools.partial(dispatch_kernel, ctxs),
        out_shape=jax.ShapeDtypeStruct((4, groups, rows, width), x.dtype),
        in_specs=specs("v"),
        out_specs=specs("v")[0],
        scratch_shapes=sems,
        compiler_params=pltpu.CompilerParams(
            collective_id=ident, has_side_effects=True, vmem_limit_bytes=40 * 2**20
        ),
        name="dispatch",
    )(x)


def combine_kernel(ctxs, x_ref, out_ref, got, half, crossed, total,
                   near_send, near_recv, far_send, far_recv, send, recv):
    groups = x_ref.shape[1]
    mine, pair, across, diagonal = tensor_peers()
    me = lax.axis_index("dp") * ctxs + lax.axis_index("ctx")
    group_meet(me, groups, ctxs, pair, across)

    def near(k, g, which, block):
        return remote(x_ref.at[block, g], got.at[which, k], near_send.at[which, k],
                      near_recv.at[which, k], {"tensor": pair})

    def far(k):
        return remote(half.at[k], crossed.at[k], far_send.at[k], far_recv.at[k],
                      {"tensor": across})

    def shipment(k):
        return remote(total.at[k], out_ref.at[me], send.at[k], recv.at[k],
                      group_target(lax.rem(me + k, groups), ctxs))

    def begin(k, carry):
        g = lax.rem(me + k, groups)
        near(k, g, 0, diagonal).start()
        near(k, g, 1, pair).start()
        return carry

    lax.fori_loop(0, groups, begin, 0)

    def cross(k, carry):
        g = lax.rem(me + k, groups)
        near(k, g, 0, diagonal).wait_recv()
        half[k] = (x_ref[across, g].astype(F32) + got[0, k].astype(F32)).astype(BF16)
        far(k).start()
        return carry

    lax.fori_loop(0, groups, cross, 0)

    def add(k):
        g = lax.rem(me + k, groups)
        near(k, g, 1, pair).wait_recv()
        far(k).wait_recv()
        return (
            x_ref[mine, g].astype(F32) + got[1, k].astype(F32) + crossed[k].astype(F32)
        ).astype(BF16)

    def ship(k, carry):
        total[k] = add(k)
        shipment(k).start()
        return carry

    out_ref[me] = add(0)
    lax.fori_loop(1, groups, ship, 0)

    def finish(k, carry):
        g = lax.rem(me + k, groups)
        near(k, g, 0, diagonal).wait_send()
        near(k, g, 1, pair).wait_send()
        far(k).wait_send()
        return carry

    lax.fori_loop(0, groups, finish, 0)

    def land(k, carry):
        shipment(k).wait_recv()
        shipment(k).wait_send()
        return carry

    lax.fori_loop(1, groups, land, 0)


def combine(x, ctxs, ident):
    _, groups, rows, width = x.shape
    block = (groups, rows, width)
    one = pltpu.SemaphoreType.DMA((groups,))
    two = pltpu.SemaphoreType.DMA((2, groups))
    return pl.pallas_call(
        functools.partial(combine_kernel, ctxs),
        out_shape=jax.ShapeDtypeStruct(block, BF16),
        in_specs=specs("v"),
        out_specs=specs("v")[0],
        scratch_shapes=[
            pltpu.VMEM((2,) + block, BF16),
            pltpu.VMEM(block, BF16),
            pltpu.VMEM(block, BF16),
            pltpu.VMEM(block, BF16),
            two, two, one, one, one, one,
        ],
        compiler_params=pltpu.CompilerParams(
            collective_id=ident, has_side_effects=True, vmem_limit_bytes=52 * 2**20
        ),
        name="combine",
    )(x)


def all_meet(me, groups, ctxs, mine):
    barrier = pltpu.get_barrier_semaphore()

    def greet(k, carry):
        pl.semaphore_signal(
            barrier, inc=1, device_id=group_target(lax.rem(me + k, groups), ctxs),
            device_id_type=pl.DeviceIdType.MESH,
        )
        return carry

    lax.fori_loop(1, groups, greet, 0)
    for k in range(1, 4):
        pl.semaphore_signal(
            barrier, inc=1, device_id={"tensor": lax.rem(mine + k, 4)},
            device_id_type=pl.DeviceIdType.MESH,
        )
    pl.semaphore_wait(barrier, groups + 2)


def spread(out_ref, dps, ctxs, send, recv, side_send, side_recv):
    at_dp, at_ctx = lax.axis_index("dp"), lax.axis_index("ctx")

    def along(k):
        block = out_ref.at[at_dp * ctxs + at_ctx]
        return remote(block, block, send.at[k], recv.at[k], {"dp": lax.rem(at_dp + k, dps)})

    def side(k, c):
        block = out_ref.at[lax.rem(at_dp + dps - k, dps) * ctxs + at_ctx]
        return remote(block, block, side_send.at[k, c], side_recv.at[k, c],
                      {"ctx": lax.rem(at_ctx + c, ctxs)})

    for k in range(1, dps):
        along(k).start()
    for k in range(dps):
        if k:
            along(k).wait_recv()
        for c in range(1, ctxs):
            side(k, c).start()
    for k in range(dps):
        for c in range(1, ctxs):
            side(k, c).wait_recv()
            side(k, c).wait_send()
        if k:
            along(k).wait_send()


def spread_sems(dps, ctxs):
    line, plane = pltpu.SemaphoreType.DMA((dps,)), pltpu.SemaphoreType.DMA((dps, ctxs))
    return [line, line, plane, plane]


def group_gather_kernel(dps, ctxs, x_ref, out_ref, *sems):
    me = lax.axis_index("dp") * ctxs + lax.axis_index("ctx")
    all_meet(me, dps * ctxs, ctxs, lax.axis_index("tensor"))
    out_ref[me] = x_ref[...]
    spread(out_ref, dps, ctxs, *sems)


def group_gather(x, dps, ctxs, ident):
    rows, width = x.shape
    out = pl.pallas_call(
        functools.partial(group_gather_kernel, dps, ctxs),
        out_shape=jax.ShapeDtypeStruct((dps * ctxs, rows, width), x.dtype),
        in_specs=specs("v"),
        out_specs=specs("v")[0],
        scratch_shapes=spread_sems(dps, ctxs),
        compiler_params=pltpu.CompilerParams(
            collective_id=ident, has_side_effects=True, vmem_limit_bytes=32 * 2**20
        ),
        name="group_gather",
    )(x)
    return out.reshape(dps * ctxs * rows, width)


def group_sum_kernel(dps, ctxs, w_ref, s_ref, out_ref, small_ref, got, across, near, far,
                     send, recv, t_send, t_recv, s_send, s_recv, *sems):
    groups = dps * ctxs
    me = lax.axis_index("dp") * ctxs + lax.axis_index("ctx")
    mine = lax.axis_index("tensor")
    all_meet(me, groups, ctxs, mine)

    def small(k):
        return remote(s_ref, across.at[k], t_send.at[k], t_recv.at[k],
                      {"tensor": lax.rem(mine + k, 4)})

    def block(k):
        to = lax.rem(me + k, groups)
        return remote(w_ref.at[to], got.at[k], send.at[k], recv.at[k], group_target(to, ctxs))

    def tiny(k):
        return remote(near, far.at[k], s_send.at[k], s_recv.at[k],
                      group_target(lax.rem(me + k, groups), ctxs))

    def start_tiny(k, carry):
        tiny(k).start()
        return carry

    def start_block(k, carry):
        block(k).start()
        return carry

    for k in range(1, 4):
        small(k).start()
    lax.fori_loop(1, groups, start_block, 0)
    total = s_ref[...].astype(F32)
    for k in range(1, 4):
        small(k).wait_recv()
        total = total + across[k].astype(F32)
    near[...] = total.astype(BF16)
    lax.fori_loop(1, groups, start_tiny, 0)

    def add(k, acc):
        block(k).wait_recv()
        return acc + got[k].astype(F32)

    out_ref[me] = lax.fori_loop(1, groups, add, w_ref[me].astype(F32)).astype(BF16)
    spread(out_ref, dps, ctxs, *sems)

    def add_tiny(k, acc):
        tiny(k).wait_recv()
        return acc + far[k].astype(F32)

    small_ref[...] = lax.fori_loop(1, groups, add_tiny, near[...].astype(F32))

    def leave(k, carry):
        block(k).wait_send()
        tiny(k).wait_send()
        return carry

    lax.fori_loop(1, groups, leave, 0)
    for k in range(1, 4):
        small(k).wait_send()


def group_sum(grads, small, dps, ctxs, ident):
    groups = dps * ctxs
    rows, width = grads.shape
    block = (groups, rows // groups, width)
    line = pltpu.SemaphoreType.DMA((groups,))
    four = pltpu.SemaphoreType.DMA((4,))
    out, total = pl.pallas_call(
        functools.partial(group_sum_kernel, dps, ctxs),
        out_shape=(
            jax.ShapeDtypeStruct(block, BF16), jax.ShapeDtypeStruct(small.shape, F32),
        ),
        in_specs=specs("v", "v"),
        out_specs=tuple(specs("v", "v")),
        scratch_shapes=[
            pltpu.VMEM(block, BF16),
            pltpu.VMEM((4,) + small.shape, BF16),
            pltpu.VMEM(small.shape, BF16),
            pltpu.VMEM((groups,) + small.shape, BF16),
            line, line, four, four, line, line,
        ] + spread_sems(dps, ctxs),
        compiler_params=pltpu.CompilerParams(
            collective_id=ident, has_side_effects=True, vmem_limit_bytes=48 * 2**20
        ),
        name="group_sum",
    )(grads.astype(BF16).reshape(block), small)
    return out.reshape(rows, width).astype(F32), total


def halve(x):
    width = x.shape[-1] // 2
    return jnp.concatenate([x[..., :width], x[..., width:]], axis=-2)


def unhalve(x):
    rows = x.shape[-2] // 2
    return jnp.concatenate([x[..., :rows, :], x[..., rows:, :]], axis=-1)


def table_grad(diag, starts):
    heads, blocks, sub, span = diag.shape
    delta = lax.broadcasted_iota(jnp.int32, (blocks, sub, span), 0)
    row = lax.broadcasted_iota(jnp.int32, (blocks, sub, span), 1)
    lane = lax.broadcasted_iota(jnp.int32, (blocks, sub, span), 2)
    far = lane_distance(delta, span // 2, lane) + row
    later = jnp.concatenate([starts[1:], jnp.full((1,), 2**30, jnp.int32)])
    inside = (far[None] >= starts[:, None, None, None]) & (far[None] < later[:, None, None, None])
    return jnp.sum(
        jnp.where(inside[:, None], diag[None], 0.0), axis=(2, 3, 4)
    )


def hi_lo(x):
    hi = x.astype(BF16)
    return hi, (x - hi.astype(F32)).astype(BF16)


def norm_scale(value):
    return lax.rsqrt(jnp.mean(value * value, axis=-1, keepdims=True) + EPS)


def norm_backward(value, scale, gain, grad_normed):
    scaled = grad_normed * gain
    grad_value = scale * scaled - value * scale**3 * jnp.mean(
        value * scaled, axis=-1, keepdims=True
    )
    return grad_value, jnp.sum(grad_normed * value * scale, axis=0)


def on_device(
    inputs, gain_attention, w_query, w_key, w_value, w_output, bias_table, bucket_start,
    gain_experts, w_router, w_up, w_down, expert_ids, slot_index, cotangent,
):
    sequences, rows, width = inputs.shape
    tokens = sequences * rows
    experts = w_router.shape[1]
    top = expert_ids.shape[2]
    capacity = 5 * tokens * top // (4 * experts)
    heads = bias_table.shape[1]
    split = lax.axis_size("tensor")
    ctxs = lax.axis_size("ctx")
    dps = lax.axis_size("dp")
    at_tensor = lax.axis_index("tensor")
    at_ctx = lax.axis_index("ctx")
    me = at_ctx.astype(jnp.int32).reshape(1)
    part = tokens // split
    slots = (capacity // split + 7) // 8 * 8
    own = capacity // split
    shard_rows = experts * slots
    groups = ("dp", "ctx")

    def my_tokens(x):
        return lax.dynamic_slice_in_dim(x, at_tensor * part, part, 0)

    route = expert_ids.reshape(tokens, top)
    place = slot_index.reshape(tokens, top)
    local = place - at_tensor * own
    inside = (place >= 0) & (local >= 0) & (local < own)
    row_of = jnp.where(inside, route * slots + local, -1)
    spots = jnp.arange(shard_rows, dtype=jnp.int32)
    hits = [row_of[:, k : k + 1] == spots[None, :] for k in range(top)]
    ones = [h.astype(BF16) for h in hits]
    any_hit = sum(ones[1:], ones[0])
    cot = cotangent.reshape(tokens, width)

    hh = w_query.shape[1]
    all_w = group_gather(
        jnp.concatenate([w_query, w_key, w_value, w_output], axis=1), dps, ctxs, 8
    )
    qkv_w, output_w = all_w[:, : 3 * hh], all_w[:, 3 * hh :]
    cot_out = dot(any_hit, cot, 0, 0).astype(BF16).reshape(experts, slots, width)
    source = inputs.astype(F32).reshape(tokens, width)
    scale_one = norm_scale(source)
    normed_one = (source * scale_one * gain_attention).astype(BF16)
    qkv = dot(normed_one, qkv_w).astype(BF16).reshape(sequences, rows, 3 * hh)
    kv_all = lax.all_gather(qkv[:, :, hh:], "ctx", axis=1, tiled=True)
    seen = [
        attend_forward(
            me, bucket_start, bias_table,
            qkv[b, :, :hh], kv_all[b, :, :hh], kv_all[b, :, hh:],
        )
        for b in range(sequences)
    ]
    mixed = jnp.concatenate([s[0] for s in seen], axis=0)
    source_mine = my_tokens(source)
    hidden = source_mine + tensor_scatter(dot(mixed, output_w, 1, 1), 0)
    scale_two = norm_scale(hidden)
    normed_mine = (hidden * scale_two * gain_experts).astype(BF16)
    normed_two = tensor_gather(normed_mine, 1)

    router_logits = dot(normed_two, w_router)
    picks = route[:, :, None] == jnp.arange(experts, dtype=jnp.int32)[None, None, :]
    chosen = jnp.sum(jnp.where(picks, router_logits[:, None, :], 0.0), axis=-1)
    gates = jax.nn.softmax(chosen, axis=-1)
    row_gate = sum(
        jnp.sum(jnp.where(hits[k], gates[:, k : k + 1], 0.0), axis=0) for k in range(top)
    )

    hi_and_lo = jnp.stack(hi_lo(row_gate.reshape(experts, slots)), axis=1)
    gate_block = jnp.pad(hi_and_lo, ((0, 0), (0, 14), (0, width // 2 - slots)))
    rows_out = dot(any_hit, normed_two, 0, 0).astype(BF16).reshape(experts, slots, width)
    arrived = dispatch(
        jnp.concatenate([halve(rows_out), gate_block, halve(cot_out)], axis=1), ctxs, 2
    )
    cot_rows = unhalve(arrived[:, :, 2 * slots + 16 :]).reshape(split * shard_rows, width)
    buffer = unhalve(arrived[:, :, : 2 * slots]).reshape(split * shard_rows, width)
    gate_rows = (
        arrived[:, :, 2 * slots, :slots].astype(F32)
        + arrived[:, :, 2 * slots + 1, :slots].astype(F32)
    ).reshape(split * shard_rows, 1)
    grad_produced = (gate_rows * cot_rows.astype(F32)).astype(BF16)
    up, down = w_up[0], w_down[0]
    before = dot(buffer, up)
    activated, gelu_pullback = jax.vjp(jax.nn.gelu, before)
    activated = activated.astype(BF16)
    partial_out = dot(activated, down).astype(BF16)
    grad_before = gelu_pullback(dot(grad_produced, down, 1, 1))[0].astype(BF16)
    partial_grad = dot(grad_before, up, 1, 1).astype(BF16)
    shares = (split, experts, slots, width)
    came_back = combine(
        jnp.concatenate(
            [halve(partial_out.reshape(shares)), halve(partial_grad.reshape(shares))], axis=2
        ),
        ctxs, 3,
    )
    returned = unhalve(came_back[:, : 2 * slots]).reshape(shard_rows, width)
    grad_returned = unhalve(came_back[:, 2 * slots :]).reshape(shard_rows, width)
    grad_down = dot(activated, grad_produced, 0, 0)
    grad_up = dot(buffer, grad_before, 0, 0)

    cot32 = cot.astype(F32)
    picked = [dot(one, returned) for one in ones]
    mixture = sum(gates[:, k : k + 1] * picked[k] for k in range(top))
    gate_part = jnp.stack([jnp.sum(cot32 * picked[k], axis=-1) for k in range(top)], axis=1)
    part_hi, part_lo = hi_lo(gate_part)
    summed = tensor_scatter(
        jnp.concatenate(
            [
                mixture.astype(BF16),
                dot(any_hit, grad_returned).astype(BF16),
                jnp.pad(jnp.concatenate([part_hi, part_lo], axis=1), ((0, 0), (0, 128 - 2 * top))),
            ],
            axis=1,
        ),
        4,
    )
    result = hidden + summed[:, :width]
    grad_gates = (
        summed[:, 2 * width : 2 * width + top] + summed[:, 2 * width + top : 2 * width + 2 * top]
    )
    gates_mine = my_tokens(gates)
    grad_chosen = gates_mine * (
        grad_gates - jnp.sum(gates_mine * grad_gates, axis=-1, keepdims=True)
    )
    grad_logits = jnp.sum(
        jnp.where(my_tokens(picks), grad_chosen[:, :, None], 0.0), axis=1
    ).astype(BF16)
    grad_router = dot(normed_mine, grad_logits, 0, 0)
    grad_normed_two = summed[:, width : 2 * width] + dot(grad_logits, w_router, 1, 1)
    grad_back, grad_gain_two = norm_backward(hidden, scale_two, gain_experts, grad_normed_two)
    grad_hidden = my_tokens(cot).astype(F32) + grad_back
    grad_branch = tensor_gather(grad_hidden.astype(BF16), 5)

    grad_mixed = dot(grad_branch, output_w).astype(BF16).reshape(sequences, rows, hh)
    grad_output = dot(grad_branch, mixed, 0, 0)
    back = [
        attend_backward(
            me, bucket_start, bias_table,
            qkv[b, :, :hh], kv_all[b, :, :hh], kv_all[b, :, hh:],
            grad_mixed[b], seen[b][1], seen[b][2],
        )
        for b in range(sequences)
    ]
    kv_part = jnp.stack([jnp.concatenate([b[1], b[2]], axis=1) for b in back])
    kv_grad = lax.psum_scatter(kv_part, "ctx", scatter_dimension=1, tiled=True)
    qkv_grad = jnp.concatenate([jnp.stack([b[0] for b in back]), kv_grad], axis=2).reshape(
        tokens, 3 * hh
    )
    grad_table = sum(table_grad(b[3], bucket_start) for b in back)
    grad_normed_one = tensor_scatter(dot(qkv_grad, qkv_w, 1, 1), 6)
    grad_back_one, grad_gain_one = norm_backward(
        source_mine, my_tokens(scale_one), gain_attention, grad_normed_one
    )
    ends = tensor_gather(
        jnp.concatenate([(grad_hidden + grad_back_one).astype(BF16), result.astype(BF16)], axis=1),
        7,
    )
    grad_inputs, layer_out = ends[:, :width].astype(F32), ends[:, width:]

    flat_table = jnp.pad(
        grad_table.reshape(1, -1), ((0, 0), (0, width - grad_table.size))
    )
    flat_table = jnp.roll(flat_table, at_tensor * grad_table.size, axis=1)
    rows_small = jnp.concatenate(
        [grad_gain_one[None], grad_gain_two[None], grad_router.T, flat_table], axis=0
    ).astype(BF16)
    rows_small = jnp.pad(rows_small, ((0, -rows_small.shape[0] % 16), (0, 0)))
    grads, small = group_sum(
        jnp.concatenate([dot(normed_one, qkv_grad, 0, 0), grad_output], axis=1),
        rows_small, dps, ctxs, 9,
    )
    grad_table = lax.dynamic_slice_in_dim(
        small[2 + experts], at_tensor * grad_table.size, grad_table.size, 0
    ).reshape(grad_table.shape)
    return (
        layer_out.reshape(sequences, rows, width),
        grad_inputs.reshape(sequences, rows, width),
        small[0],
        grads[:, :hh],
        grads[:, hh : 2 * hh],
        grads[:, 2 * hh : 3 * hh],
        grads[:, 3 * hh :],
        grad_table,
        small[1],
        small[2 : 2 + experts].T,
        grad_up[None],
        grad_down[None],
    )


def solution(mesh):
    in_specs = (
        P("dp", "ctx", None),
        P(),
        P(("dp", "ctx"), "tensor"),
        P(("dp", "ctx"), "tensor"),
        P(("dp", "ctx"), "tensor"),
        P(("dp", "ctx"), "tensor"),
        P(None, "tensor"),
        P(),
        P(),
        P(),
        P(("dp", "ctx"), None, "tensor"),
        P(("dp", "ctx"), "tensor", None),
        P("dp", "ctx", None),
        P("dp", "ctx", None),
        P("dp", "ctx", None),
    )
    out_specs = (
        P("dp", "ctx", None),
        P("dp", "ctx", None),
        P(),
        P(None, "tensor"),
        P(None, "tensor"),
        P(None, "tensor"),
        P(None, "tensor"),
        P(None, "tensor"),
        P(),
        P(),
        P(("dp", "ctx"), None, "tensor"),
        P(("dp", "ctx"), "tensor", None),
    )
    return jax.shard_map(
        on_device, mesh=mesh, in_specs=in_specs, out_specs=out_specs, check_vma=False
    )
```
